256 devices in a mesh: hist: 32 (over y_hi, z, core), tensor: 8 (over y_lo, x).
Axes of the slice: x: 4, y: 4 (y_hi: 2, y_lo: 2; y = y_hi * 2 + y_lo), z: 8, core: 2. Of those that a mesh axis runs over, the one named last changes fastest.
Arguments:
- latents: bfloat16 [8, 1024, 2048], P(None, 'hist'), may hold values from -5 to 5
- keys: bfloat16 [8, 2048, 2048], P(None, 'hist', 'tensor'), may hold values from -5 to 5
- values: bfloat16 [8, 2048, 2048], P(None, 'hist', 'tensor'), may hold values from -24 to 24
- cutoff: int32 [8, 1024], replicated, may hold values from 1 to 2048, as said below
- w_q_cross: bfloat16 [2048, 2048], P(None, 'tensor'), may hold values from -2 to 2
- w_o_cross: bfloat16 [2048, 2048], P('tensor'), may hold values from -0.125 to 0.125
- w_qkv_self: bfloat16 [3, 2048, 2048], P(None, None, 'tensor'), may hold values from -1 to 1
- w_o_self: bfloat16 [2048, 2048], P('tensor'), may hold values from -0.125 to 0.125
- w_up: bfloat16 [2048, 4096], P(None, 'tensor'), may hold values from -0.125 to 0.125
- w_down: bfloat16 [4096, 2048], P('tensor'), may hold values from -0.09375 to 0.09375
Outputs:
- encoded: bfloat16 [8, 1024, 2048], P(None, 'hist', 'tensor')
The draws below stay inside these ranges and needn't reach their ends.
Inputs may be any that keep to these rules, and one draw needn't show every extreme that they name: cutoff[b, i] counts the first history messages of sequence b that latent i sees, and it is at most 2(i + 1), since latent i stands at history position 2i + 1 and sees nothing after it; the last latent of every sequence sees all 2048.
All inputs are finite; a program needn't handle non-finite values.
Results may differ from the reference program's by a relative error of at most 0.025.
Values may be sent and summed in bfloat16 or wider, within the bound.
A program may use at most 128 MiB of HBM per device.

```python
import math
import jax
import jax.numpy as jnp
from jax import lax

D = 2048
HEADS = 16
HD = 128
FF = 4096
SEQS = 8
LAT = 1024
HIST = 2048


def sign_vector(key, number, entries):
    coins = jax.random.bernoulli(jax.random.fold_in(key, number), 0.5, (entries,))
    return jnp.where(coins, 1.0, -1.0).astype(jnp.float32)


def shared_signs(key):
    return (sign_vector(key, 101, D), sign_vector(key, 102, D), sign_vector(key, 103, D), sign_vector(key, 104, D))


def draw_cutoff(key, part):
    key = jax.random.fold_in(key, 7)
    lagging = jax.random.randint(key, (SEQS, LAT), 0, max(HIST // 4, 1))
    places = jnp.arange(LAT, dtype=jnp.int32)
    reach = (places + 1) * HIST // LAT
    lagging = jnp.where(places[None, :] == LAT - 1, 0, lagging)
    return jnp.clip(reach[None, :] - lagging, 1, HIST).astype(jnp.int32)


def draw_latents(key, part):
    signs = shared_signs(key)
    key = jax.random.fold_in(key, 11)
    kind_key, cross_key, self_key, noise_key = jax.random.split(key, 4)
    kinds = jax.random.randint(kind_key, (SEQS, LAT), 0, 4)
    cross_strength = jnp.where(kinds == 0, jax.random.uniform(cross_key, (SEQS, LAT), jnp.float32, 0.4, 1.2), 0.0)
    self_strength = jnp.where(kinds == 1, jax.random.uniform(self_key, (SEQS, LAT), jnp.float32, 0.6, 1.5), 0.0)
    noise = 0.5 * jnp.clip(jax.random.normal(noise_key, (SEQS, LAT, D), jnp.float32), -6.0, 6.0)
    return (noise + cross_strength[..., None] * signs[0] + self_strength[..., None] * signs[1]).astype(jnp.bfloat16)


def draw_keys(key, part):
    signs = shared_signs(key)
    key = jax.random.fold_in(key, 13)
    pick_key, noise_key, small_key = jax.random.split(key, 3)
    chosen = jax.random.bernoulli(pick_key, 0.25, (SEQS, HIST))
    noise = jnp.clip(jax.random.normal(noise_key, (SEQS, HIST, D), jnp.float32), -5.0, 5.0)
    small = 0.2 * jnp.clip(jax.random.normal(small_key, (SEQS, HIST, D), jnp.float32), -1.0, 1.0)
    planted = 3.0 * signs[2] + small
    return jnp.where(chosen[..., None], planted, noise).astype(jnp.bfloat16)


def draw_w_q_cross(key, part):
    signs = shared_signs(key)
    key = jax.random.fold_in(key, 17)
    base = jnp.clip(jax.random.normal(key, (D, D), jnp.float32), -4.0, 4.0) * (1.0 / math.sqrt(D))
    strength = 93.0 / math.sqrt(HD)
    return (base + strength / D * signs[0][:, None] * signs[2][None, :]).astype(jnp.bfloat16)


def draw_w_qkv_self(key, part):
    signs = shared_signs(key)
    key = jax.random.fold_in(key, 19)
    base = jnp.clip(jax.random.normal(key, (3, D, D), jnp.float32), -4.0, 4.0) * (1.0 / math.sqrt(D))
    strength = math.sqrt(400.0 / math.sqrt(HD))
    planted = strength / D * signs[1][:, None] * signs[3][None, :]
    chosen = jnp.array([1.0, 1.0, 0.0], jnp.float32)[:, None, None]
    return (base + chosen * planted[None, :, :]).astype(jnp.bfloat16)


def block_levels(own_key, dims, cuts, low, high):
    def one(dim, blocks):
        steps = jax.random.uniform(jax.random.fold_in(jax.random.fold_in(own_key, 6), dim), (blocks,), jnp.float32, low / len(cuts), high / len(cuts))
        return jnp.repeat(jnp.exp(steps), dims[dim] // blocks).reshape((-1,) + (1,) * (len(dims) - dim - 1))

    level = one(*cuts[0])
    for cut in cuts[1:]:
        level = level * one(*cut)
    return level


def centred(rng, shape, width, limit, cuts=(), kind=jnp.bfloat16):
    level = block_levels(rng, shape, cuts, -0.22, 0.18) if cuts else 1.0
    values = jax.random.normal(rng, shape, jnp.float32) * width * level
    return jnp.minimum(jnp.maximum(values, -limit), limit).astype(kind)


def setup_inputs(seed: int = 0) -> dict:
    seeds = jax.random.split(jax.random.key(seed), 11)
    latents = draw_latents(jax.random.fold_in(seeds[10], 71), 0)
    keys = draw_keys(jax.random.fold_in(seeds[10], 71), 0)
    values = centred(seeds[2], (SEQS, HIST, D), 4.0, 24.0, ((1, 32), (2, 8)))
    cutoff = draw_cutoff(jax.random.fold_in(seeds[10], 71), 0)
    w_q_cross = draw_w_q_cross(jax.random.fold_in(seeds[10], 71), 0)
    w_o_cross = centred(seeds[5], (D, D), D ** -0.5, 0.125, ((0, 8),))
    w_qkv_self = draw_w_qkv_self(jax.random.fold_in(seeds[10], 71), 0)
    w_o_self = centred(seeds[7], (D, D), D ** -0.5, 0.125, ((0, 8),))
    w_up = centred(seeds[8], (D, FF), D ** -0.5, 0.125, ((1, 8),))
    w_down = centred(seeds[9], (FF, D), FF ** -0.5, 0.09375, ((0, 8),))
    return dict(latents=latents, keys=keys, values=values, cutoff=cutoff, w_q_cross=w_q_cross, w_o_cross=w_o_cross, w_qkv_self=w_qkv_self, w_o_self=w_o_self, w_up=w_up, w_down=w_down)


EPSILON = 1e-06
MASKED = -1e+30

def rms_rows(values):
    wide = values.astype(jnp.float32)
    return (wide * lax.rsqrt(lax.optimization_barrier(jnp.mean(wide * wide, axis=-1, keepdims=True)) + EPSILON)).astype(jnp.bfloat16)

def attend(query, keys, values, visible):
    scores = jnp.einsum('qhe,khe->qhk', query.astype(jnp.float32), keys.astype(jnp.float32)) * (1.0 / math.sqrt(HD))
    scores = jnp.where(visible[:, None, :], scores, MASKED)
    largest = lax.optimization_barrier(jnp.max(scores, axis=-1, keepdims=True))
    weights = jnp.where(visible[:, None, :], jnp.exp(scores - largest), 0.0)
    total = lax.optimization_barrier(jnp.sum(weights, axis=-1))
    summed = jnp.einsum('qhk,khe->qhe', weights.astype(jnp.bfloat16).astype(jnp.float32), values.astype(jnp.float32))
    return (summed / total[..., None]).astype(jnp.bfloat16)

def project(left, right):
    return jnp.dot(left, right, preferred_element_type=jnp.float32)

def reference(latents, keys, values, cutoff, w_q_cross, w_o_cross, w_qkv_self, w_o_self, w_up, w_down):
    flat = latents.reshape(SEQS * LAT, D)
    query = project(rms_rows(flat), w_q_cross).astype(jnp.bfloat16).reshape(SEQS, LAT, HEADS, HD)
    history = jnp.arange(HIST, dtype=jnp.int32)

    def cross_one(items):
        query_seq, key_seq, value_seq, cut_seq = items
        visible = history[None, :] < cut_seq[:, None]
        return attend(query_seq, key_seq.reshape(HIST, HEADS, HD), value_seq.reshape(HIST, HEADS, HD), visible)
    context = lax.map(cross_one, (query, keys, values, cutoff)).reshape(SEQS * LAT, D)
    first = (flat.astype(jnp.float32) + project(context, w_o_cross)).astype(jnp.bfloat16)
    normed_two = rms_rows(first)
    self_query, self_keys, self_values = [project(normed_two, w_qkv_self[index]).astype(jnp.bfloat16).reshape(SEQS, LAT, HEADS, HD) for index in range(3)]
    places = jnp.arange(LAT, dtype=jnp.int32)
    causal = places[None, :] <= places[:, None]

    def self_one(items):
        query_seq, key_seq, value_seq = items
        return attend(query_seq, key_seq, value_seq, causal)
    mixed = lax.map(self_one, (self_query, self_keys, self_values)).reshape(SEQS * LAT, D)
    second = (first.astype(jnp.float32) + project(mixed, w_o_self)).astype(jnp.bfloat16)
    hidden = jax.nn.gelu(project(rms_rows(second), w_up)).astype(jnp.bfloat16)
    encoded = (second.astype(jnp.float32) + project(hidden, w_down)).astype(jnp.bfloat16)
    return encoded.reshape(SEQS, LAT, D)
```

```python
import functools
import math

import jax
import jax.numpy as jnp
from jax import lax
from jax.experimental import pallas as pl
from jax.experimental.pallas import tpu as pltpu
from jax.sharding import PartitionSpec as P

HD = 128
EPSILON = 1e-06
MASKED = -1e30
MESH = pl.DeviceIdType.MESH
BF = jnp.bfloat16
F32 = jnp.float32
SCALE = math.log2(math.e) / math.sqrt(HD)


def dot(left, right):
    return jnp.dot(left, right, preferred_element_type=F32)


def dot_t(left, right):
    return lax.dot_general(left, right, (((1,), (1,)), ((), ())), preferred_element_type=F32)


def remote(src, dst, send_sem, recv_sem, hist, tensor):
    return pltpu.make_async_remote_copy(
        src_ref=src,
        dst_ref=dst,
        send_sem=send_sem,
        recv_sem=recv_sem,
        device_id=(hist, tensor),
        device_id_type=MESH,
    )


def attend(query, pieces):
    scores = [jnp.where(seen, dot_t(query, keys) * SCALE, MASKED) for keys, _, seen in pieces]
    largest = functools.reduce(jnp.maximum, [jnp.max(s, axis=-1, keepdims=True) for s in scores])
    total = jnp.zeros_like(largest)
    summed = jnp.zeros((query.shape[0], HD), F32)
    for score, (_, values, _) in zip(scores, pieces):
        weights = jnp.exp2(score - largest)
        total = total + jnp.sum(weights, axis=-1, keepdims=True)
        summed = summed + dot(weights.astype(BF), values)
    return (summed / total).astype(BF)


def step_kernel(
    sizes,
    lat_hbm, keys_hbm, values_hbm, cut_ref, wq_hbm, wo_hbm, wqkv_hbm, wos_hbm, wup_hbm, wdn_hbm,
    out_hbm,
    lat_v, wq_v, wo_v, wqkv_v, wos_v, wup_v, wdn_v,
    kv, qsend, qbuf, latres, ctxsend, ctx, send_one, recv_one, gather_one, qself, kvs, mixed,
    send_two, recv_two, gather_two, send_three, recv_three, enc,
    load_sem, kv_ssem, kv_rsem, fw_ssem, fw_rsem, q_ssem, q_rsem, lat_ssem, lat_rsem,
    ctx_ssem, ctx_rsem, rs_ssem, rs_rsem, ag_ssem, ag_rsem, kvs_ssem, kvs_rsem, out_ssem, out_rsem,
):
    chips, tensors, lat_rows, key_rows, width = sizes
    half_chips = chips // 2
    rows = half_chips * lat_rows
    cols = width // tensors
    hist = lax.axis_index("hist")
    tensor = lax.axis_index("tensor")
    core = lax.rem(hist, 2)
    chip = hist // 2
    other_core = 1 - core
    sibling = 2 * chip + other_core
    head = lax.rem(chip, 2)
    seq = chip // 2
    upper = chip // half_chips
    pair = 2 * (chip + 1 - 2 * head) + core

    def column(index, size):
        return pl.ds(pl.multiple_of(index * size, size), size)

    loads = [
        pltpu.make_async_copy(src, dst, load_sem.at[n])
        for n, (src, dst) in enumerate(
            [(lat_hbm, lat_v), (wq_hbm, wq_v), (wo_hbm, wo_v), (wqkv_hbm, wqkv_v),
             (wos_hbm, wos_v), (wup_hbm, wup_v), (wdn_hbm, wdn_v)]
        )
    ]
    for load in loads:
        load.start()

    barrier = pltpu.get_barrier_semaphore()

    @pl.loop(1, chips)
    def _(k):
        to = 2 * lax.rem(chip + k, chips) + core
        pl.semaphore_signal(barrier, inc=1, device_id=(to, tensor), device_id_type=MESH)

    @pl.loop(1, tensors)
    def _(k):
        to = lax.rem(tensor + k, tensors)
        pl.semaphore_signal(barrier, inc=1, device_id=(hist, to), device_id_type=MESH)

    pl.semaphore_signal(barrier, inc=1, device_id=(sibling, tensor), device_id_type=MESH)
    pl.semaphore_wait(barrier, chips - 1 + tensors - 1 + 1)

    def kv_copy(k, which, array):
        to = lax.rem(chip + k, chips)
        return remote(
            array.at[to // 2, :, column(lax.rem(to, 2), HD)],
            kv.at[core, which, pl.ds(pl.multiple_of(k * key_rows, key_rows), key_rows)],
            kv_ssem.at[which, k], kv_rsem.at[which, k], 2 * to + core, tensor,
        )

    def kv_own(which, array):
        return pltpu.make_async_copy(
            array.at[seq, :, column(head, HD)],
            kv.at[core, which, pl.ds(0, key_rows)],
            kv_rsem.at[which, 0],
        )

    kv_own(0, keys_hbm).start()
    kv_own(1, values_hbm).start()

    @pl.loop(1, chips)
    def _(k):
        kv_copy(k, 0, keys_hbm).start()
        kv_copy(k, 1, values_hbm).start()

    loads[0].wait()
    loads[1].wait()
    flat = lat_v[...].reshape(rows, width)
    wide = flat.astype(F32)
    factor = lax.rsqrt(jnp.mean(wide * wide, axis=-1, keepdims=True) + EPSILON)
    query = (dot(flat, wq_v[...]) * factor).astype(BF)
    qsend[...] = query.reshape(half_chips, lat_rows, cols)

    def q_copy(k):
        to = lax.rem(chip + k, chips)
        return remote(
            qsend.at[to // 2, :, column(lax.rem(to, 2), HD)],
            qbuf.at[pl.ds(pl.multiple_of(chip * lat_rows, lat_rows), lat_rows)],
            q_ssem.at[k], q_rsem.at[k], 2 * to + core, tensor,
        )

    q_own = pltpu.make_async_copy(
        qsend.at[seq, :, column(head, HD)],
        qbuf.at[pl.ds(pl.multiple_of(chip * lat_rows, lat_rows), lat_rows)],
        q_rsem.at[0],
    )
    q_own.start()

    @pl.loop(1, chips)
    def _(k):
        q_copy(k).start()

    def lat_copy(k):
        to_seq = lax.rem(seq + k, half_chips)
        return remote(
            lat_hbm.at[to_seq, :, column(tensor, cols)],
            latres.at[pl.ds(pl.multiple_of((chip - upper * half_chips) * lat_rows, lat_rows), lat_rows)],
            lat_ssem.at[k], lat_rsem.at[lax.rem(chip, half_chips)],
            2 * (2 * to_seq + upper) + core, tensor,
        )

    lat_own = pltpu.make_async_copy(
        lat_hbm.at[seq, :, column(tensor, cols)],
        latres.at[pl.ds(pl.multiple_of((chip - upper * half_chips) * lat_rows, lat_rows), lat_rows)],
        lat_rsem.at[lax.rem(chip, half_chips)],
    )

    @pl.when(upper == head)
    def _():
        lat_own.start()

    @pl.when(upper != head)
    def _():
        lat_copy(0).start()

    @pl.loop(1, half_chips)
    def _(k):
        lat_copy(k).start()

    step = chips // 4
    piece = step * key_rows

    def forward(n, which):
        place = kv.at[core, which, pl.ds(pl.multiple_of(n * piece, piece), piece)]
        return remote(place, place, fw_ssem.at[which, n], fw_rsem.at[which, n], sibling, tensor)

    kv_own(0, keys_hbm).wait()
    kv_own(1, values_hbm).wait()

    @pl.loop(0, 4)
    def _(n):
        @pl.loop(0, step)
        def _(j):
            k = n * step + j

            @pl.when(k > 0)
            def _():
                kv_copy(k, 0, keys_hbm).wait_recv()
                kv_copy(k, 1, values_hbm).wait_recv()

        forward(n, 0).start()
        forward(n, 1).start()

    q_own.wait()

    @pl.loop(1, chips)
    def _(k):
        q_copy(k).wait_recv()

    @pl.loop(0, 4)
    def _(n):
        forward(n, 0).wait_recv()
        forward(n, 1).wait_recv()

    count = chips * key_rows
    block = rows // 2

    def history_place(of_core):
        local = lax.broadcasted_iota(jnp.int32, (block, count), 1)
        source = chip - local // key_rows
        source = jnp.where(source < 0, source + chips, source)
        return (2 * source + of_core) * key_rows + lax.rem(local, key_rows)

    def cross(start):
        at = pl.ds(pl.multiple_of(start, block), block)
        cut = cut_ref[at, :]
        return attend(
            qbuf[at, :],
            [(kv[n, 0], kv[n, 1], history_place(n) < cut) for n in range(2)],
        )

    @pl.loop(0, 2)
    def _(n):
        ctxsend[pl.ds(pl.multiple_of(n * block, block), block), :] = cross(
            (1 - head) * rows + n * block
        )

    ctx_copy = remote(
        ctxsend, ctx.at[:, column(head, HD)], ctx_ssem, ctx_rsem, pair, tensor
    )
    ctx_copy.start()

    @pl.loop(0, 2)
    def _(n):
        ctx[pl.ds(pl.multiple_of(n * block, block), block), column(head, HD)] = cross(
            head * rows + n * block
        )

    ctx_copy.wait_recv()

    def rs_copy(phase, k, send, recv):
        return remote(
            send.at[k - 1], recv.at[k - 1], rs_ssem.at[phase, k], rs_rsem.at[phase, k],
            hist, lax.rem(tensor + k, tensors),
        )

    def scatter(phase, left, weight, residual, send, recv):
        for k in range(1, tensors):
            to = lax.rem(tensor + k, tensors)
            send[k - 1] = dot(left, weight[:, column(to, cols)]).astype(BF)
            rs_copy(phase, k, send, recv).start()
        total = residual + dot(left, weight[:, column(tensor, cols)])
        for k in range(1, tensors):
            rs_copy(phase, k, send, recv).wait_recv()
            total = total + recv[k - 1].astype(F32)
        return total.astype(BF)

    def ag_copy(phase, k, blocks):
        return remote(
            blocks.at[0], blocks.at[k], ag_ssem.at[phase, k], ag_rsem.at[phase, k],
            hist, lax.rem(tensor + k, tensors),
        )

    def gather(phase, blocks, weights):
        for k in range(1, tensors):
            ag_copy(phase, k, blocks).start()
        sums = [0.0 for _ in weights]
        squares = 0.0
        for k in range(tensors):
            if k:
                ag_copy(phase, k, blocks).wait_recv()
            source = lax.rem(tensor - k + tensors, tensors)
            piece = blocks[k]
            wide = piece.astype(F32)
            squares = squares + jnp.sum(wide * wide, axis=-1, keepdims=True)
            sums = [s + dot(piece, w(column(source, cols))) for s, w in zip(sums, weights)]
        factor = lax.rsqrt(squares * (1.0 / width) + EPSILON)
        return [s * factor for s in sums]

    for k in range(half_chips):
        lat_slot = latres.at[pl.ds(k * lat_rows, lat_rows)]
        pltpu.make_async_copy(lat_slot, lat_slot, lat_rsem.at[k]).wait()
    loads[2].wait()
    gather_one[0] = scatter(0, ctx[...], wo_v, latres[...].astype(F32), send_one, recv_one)
    loads[3].wait()
    self_q, self_k, self_v = gather(
        0, gather_one, [lambda at, n=n: wqkv_v[n, at, :] for n in range(3)]
    )
    kvs[0, 0] = self_k.astype(BF)
    kvs[0, 1] = self_v.astype(BF)

    def kvs_copy(which, source, slot, device):
        return remote(
            kvs.at[source, which], kvs.at[slot, which],
            kvs_ssem.at[which, slot], kvs_rsem.at[which, slot], device, tensor,
        )

    for which in range(2):
        kvs_copy(which, 0, 2, pair).start()
    for which in range(2):
        kvs_copy(which, 0, 1, sibling).start()
    qself[...] = self_q.astype(BF)
    for which in range(2):
        kvs_copy(which, 0, 2, pair).wait_recv()
        kvs_copy(which, 2, 3, sibling).start()
    for which in range(2):
        kvs_copy(which, 0, 1, sibling).wait_recv()
        kvs_copy(which, 2, 3, sibling).wait_recv()

    def latent_place(axis, of_half, of_core):
        local = lax.broadcasted_iota(jnp.int32, (rows, rows), axis)
        return (
            2 * (of_half * half_chips + local // lat_rows) + of_core
        ) * lat_rows + lax.rem(local, lat_rows)

    own_place = latent_place(0, head, core)
    for h in range(cols // HD):
        at = slice(h * HD, (h + 1) * HD)
        mixed[:, at] = attend(
            qself[:, at],
            [
                (kvs[slot, 0, :, at], kvs[slot, 1, :, at], latent_place(1, half, of) <= own_place)
                for slot, (half, of) in enumerate(
                    [(head, core), (head, other_core), (1 - head, core), (1 - head, other_core)]
                )
            ],
        )

    loads[4].wait()
    gather_two[0] = scatter(1, mixed[...], wos_v, gather_one[0].astype(F32), send_two, recv_two)
    loads[5].wait()
    (raised,) = gather(1, gather_two, [lambda at: wup_v[at, :]])
    hidden = jax.nn.gelu(raised).astype(BF)
    loads[6].wait()
    enc[...] = scatter(2, hidden, wdn_v, gather_two[0].astype(F32), send_three, recv_three)

    def out_copy(n):
        to = head * half_chips + n
        return remote(
            enc.at[pl.ds(pl.multiple_of(n * lat_rows, lat_rows), lat_rows)],
            out_hbm.at[seq], out_ssem.at[n], out_rsem.at[seq], 2 * to + core, tensor,
        )

    def out_own():
        return pltpu.make_async_copy(
            enc.at[pl.ds(pl.multiple_of(lax.rem(chip, half_chips) * lat_rows, lat_rows), lat_rows)],
            out_hbm.at[seq], out_rsem.at[seq],
        )

    @pl.loop(0, half_chips)
    def _(n):
        @pl.when(head * half_chips + n != chip)
        def _():
            out_copy(n).start()

    @pl.when(upper == head)
    def _():
        out_own().start()

    for n in range(half_chips):
        pltpu.make_async_copy(out_hbm.at[n], out_hbm.at[n], out_rsem.at[n]).wait()

    @pl.loop(0, half_chips)
    def _(n):
        @pl.when(head * half_chips + n != chip)
        def _():
            out_copy(n).wait_send()

    @pl.loop(1, chips)
    def _(k):
        kv_copy(k, 0, keys_hbm).wait_send()
        kv_copy(k, 1, values_hbm).wait_send()
        q_copy(k).wait_send()

    @pl.when(upper != head)
    def _():
        lat_copy(0).wait_send()

    @pl.loop(1, half_chips)
    def _(k):
        lat_copy(k).wait_send()

    @pl.loop(0, 4)
    def _(n):
        forward(n, 0).wait_send()
        forward(n, 1).wait_send()

    ctx_copy.wait_send()
    for phase, (send, recv) in enumerate(
        [(send_one, recv_one), (send_two, recv_two), (send_three, recv_three)]
    ):
        for k in range(1, tensors):
            rs_copy(phase, k, send, recv).wait_send()
    for phase, blocks in enumerate([gather_one, gather_two]):
        for k in range(1, tensors):
            ag_copy(phase, k, blocks).wait_send()
    for which in range(2):
        kvs_copy(which, 0, 2, pair).wait_send()
        kvs_copy(which, 0, 1, sibling).wait_send()
        kvs_copy(which, 2, 3, sibling).wait_send()


def body(latents, keys, values, cutoff, w_q, w_o, w_qkv, w_os, w_up, w_down):
    seqs, lat_rows, width = latents.shape
    key_rows, cols = keys.shape[1:]
    chips = lax.axis_size("hist") // 2
    tensors = lax.axis_size("tensor")
    half_chips = chips // 2
    rows = seqs * lat_rows
    hidden = w_up.shape[1]
    hist = lax.axis_index("hist")
    own = lax.dynamic_index_in_dim(cutoff, hist // 4, 0, keepdims=False)
    own = own.reshape(chips, 2, lat_rows)
    cut = lax.dynamic_index_in_dim(own, hist % 2, 1, keepdims=False).reshape(chips * lat_rows, 1)

    def vmem(*shape):
        return pltpu.VMEM(shape, BF)

    dma = pltpu.SemaphoreType.DMA
    any_spec = pl.BlockSpec(memory_space=pl.ANY)
    blocks = (tensors - 1, rows, cols)
    return pl.pallas_call(
        functools.partial(step_kernel, (chips, tensors, lat_rows, key_rows, width)),
        out_shape=jax.ShapeDtypeStruct((seqs, lat_rows, cols), BF),
        in_specs=[any_spec] * 3 + [pl.BlockSpec(memory_space=pltpu.VMEM)] + [any_spec] * 6,
        out_specs=any_spec,
        scratch_shapes=[
            vmem(*latents.shape), vmem(*w_q.shape), vmem(*w_o.shape), vmem(*w_qkv.shape),
            vmem(*w_os.shape), vmem(*w_up.shape), vmem(*w_down.shape),
            vmem(2, 2, chips * key_rows, HD),
            vmem(seqs, lat_rows, cols),
            vmem(chips * lat_rows, HD),
            vmem(rows, cols),
            vmem(rows, HD),
            vmem(rows, cols),
            vmem(*blocks), vmem(*blocks), vmem(tensors, rows, cols),
            vmem(rows, cols),
            vmem(4, 2, rows, cols),
            vmem(rows, cols),
            vmem(*blocks), vmem(*blocks), vmem(tensors, rows, cols),
            vmem(*blocks), vmem(*blocks),
            vmem(rows, cols),
            dma((7,)),
            dma((2, chips)), dma((2, chips)),
            dma((2, 4)), dma((2, 4)),
            dma((chips,)), dma((chips,)),
            dma((half_chips,)), dma((half_chips,)),
            dma, dma,
            dma((3, tensors)), dma((3, tensors)),
            dma((2, tensors)), dma((2, tensors)),
            dma((2, 4)), dma((2, 4)),
            dma((half_chips,)), dma((half_chips,)),
        ],
        compiler_params=pltpu.CompilerParams(
            collective_id=0, has_side_effects=True, vmem_limit_bytes=50 * 1024 * 1024
        ),
        cost_estimate=pl.CostEstimate(
            flops=8 * rows * width * cols * 5, bytes_accessed=12 * 1024 * 1024, transcendentals=0
        ),
    )(latents, keys, values, cut, w_q, w_o, w_qkv, w_os, w_up, w_down)


def solution(mesh):
    placed = (
        P(None, "hist", None),
        P(None, "hist", "tensor"),
        P(None, "hist", "tensor"),
        P(),
        P(None, "tensor"),
        P("tensor", None),
        P(None, None, "tensor"),
        P("tensor", None),
        P(None, "tensor"),
        P("tensor", None),
    )
    return jax.shard_map(
        body, mesh=mesh, in_specs=placed, out_specs=P(None, "hist", "tensor"), check_vma=False
    )
```

```python
import functools
import math

import jax
import jax.numpy as jnp
from jax import lax
from jax.experimental import pallas as pl
from jax.experimental.pallas import tpu as pltpu
from jax.sharding import PartitionSpec as P

HD = 128
EPSILON = 1e-06
MASKED = -1e30
MESH = pl.DeviceIdType.MESH
BF = jnp.bfloat16
F32 = jnp.float32
SCALE = math.log2(math.e) / math.sqrt(HD)


def dot(left, right):
    return jnp.dot(left, right, preferred_element_type=F32)


def dot_t(left, right):
    return lax.dot_general(left, right, (((1,), (1,)), ((), ())), preferred_element_type=F32)


def remote(src, dst, send_sem, recv_sem, hist, tensor):
    return pltpu.make_async_remote_copy(
        src_ref=src,
        dst_ref=dst,
        send_sem=send_sem,
        recv_sem=recv_sem,
        device_id=(hist, tensor),
        device_id_type=MESH,
    )


def attend(query, pieces):
    scores = [jnp.where(seen, dot_t(query, keys) * SCALE, MASKED) for keys, _, seen in pieces]
    largest = functools.reduce(jnp.maximum, [jnp.max(s, axis=-1, keepdims=True) for s in scores])
    total = jnp.zeros_like(largest)
    summed = jnp.zeros((query.shape[0], HD), F32)
    for score, (_, values, _) in zip(scores, pieces):
        weights = jnp.exp2(score - largest)
        total = total + jnp.sum(weights, axis=-1, keepdims=True)
        summed = summed + dot(weights.astype(BF), values)
    return (summed / total).astype(BF)


def step_kernel(
    sizes,
    lat_hbm, keys_hbm, values_hbm, cut_hbm, wq_hbm, wo_hbm, wqkv_hbm, wos_hbm, wup_hbm, wdn_hbm,
    out_hbm,
    lat_v, cut_v, wq_v, wo_v, wqkv_v, wos_v, wup_v, wdn_v,
    kv, qsend, qbuf, cut_col, run_max, run_total, run_sum, latres, ctxsend, ctx,
    partial, ysend, yrecv, xsend, xrecv, blocks, qself, kvs, mixed, enc,
    load_sem, kv_ssem, kv_rsem, fw_ssem, fw_rsem, q_ssem, q_rsem, lat_ssem, lat_rsem,
    ctx_ssem, ctx_rsem, rsy_ssem, rsy_rsem, rsx_ssem, rsx_rsem, agy_ssem, agy_rsem, agx_ssem, agx_rsem,
    kvs_ssem, kvs_rsem, out_ssem, out_rsem,
):
    chips, tensors, lat_rows, key_rows, width = sizes
    depth = chips // 2
    rows = depth * lat_rows
    part = rows // 2
    cols = width // tensors
    across = tensors // 2
    hist = lax.axis_index("hist")
    tensor = lax.axis_index("tensor")
    core = lax.rem(hist, 2)
    chip = hist // 2
    upper = chip // depth
    place_z = lax.rem(chip, depth)
    lane_y = tensor // across
    place_x = lax.rem(tensor, across)
    other_core = 1 - core
    sibling = 2 * chip + other_core
    pair = 2 * ((1 - upper) * depth + place_z) + core
    twist = core * lane_y
    own_half = lax.rem(upper + twist, 2)
    sibling_half = lax.rem(upper + other_core * lane_y, 2)
    mate_hist = 2 * (lax.rem(upper + core, 2) * depth + place_z) + core
    mate_tensor = (1 - lane_y) * across + place_x

    def column(index, size):
        return pl.ds(pl.multiple_of(index * size, size), size)

    def part_rows(half):
        return pl.ds(half * part, part)

    def x_peer(d):
        return lane_y * across + lax.rem(place_x + d, across)

    def far(k):
        j = k // 2
        dz = ((j + 1) // 2) * (2 * (j % 2) - 1)
        return lax.rem(upper + k % 2, 2) * depth + lax.rem(place_z + depth + dz, depth)

    def near(k):
        j = k // 2
        dz = ((j + 1) // 2) * (2 * (j % 2) - 1)
        return lax.rem(upper + k % 2, 2) * depth + lax.rem(place_z + depth - dz, depth)

    loads = [
        pltpu.make_async_copy(src, dst, load_sem.at[n])
        for n, (src, dst) in enumerate(
            [(lat_hbm, lat_v), (wq_hbm, wq_v), (cut_hbm, cut_v), (wo_hbm, wo_v), (wqkv_hbm, wqkv_v),
             (wos_hbm, wos_v), (wup_hbm, wup_v), (wdn_hbm, wdn_v)]
        )
    ]
    for load in loads[:3]:
        load.start()

    barrier = pltpu.get_barrier_semaphore()

    @pl.loop(1, chips)
    def _(k):
        pl.semaphore_signal(
            barrier, inc=1, device_id=(2 * near(k) + core, tensor), device_id_type=MESH
        )

    for d in range(1, across):
        pl.semaphore_signal(barrier, inc=1, device_id=(hist, x_peer(d)), device_id_type=MESH)
    pl.semaphore_signal(barrier, inc=1, device_id=(mate_hist, mate_tensor), device_id_type=MESH)
    pl.semaphore_signal(barrier, inc=1, device_id=(sibling, tensor), device_id_type=MESH)
    pl.semaphore_wait(barrier, chips - 1 + across - 1 + 2)

    def kv_copy(k, which, array):
        to = far(k)
        return remote(
            array.at[lax.rem(to, depth), :, column(to // depth, HD)],
            kv.at[core, which, pl.ds(pl.multiple_of(k * key_rows, key_rows), key_rows)],
            kv_ssem.at[which, k], kv_rsem.at[which, k], 2 * to + core, tensor,
        )

    def kv_own(which, array):
        return pltpu.make_async_copy(
            array.at[place_z, :, column(upper, HD)],
            kv.at[core, which, pl.ds(0, key_rows)],
            kv_rsem.at[which, 0],
        )

    kv_own(0, keys_hbm).start()
    kv_own(1, values_hbm).start()

    @pl.loop(1, depth)
    def _(k):
        kv_copy(k, 0, keys_hbm).start()
        kv_copy(k, 1, values_hbm).start()

    loads[0].wait()
    loads[1].wait()
    flat = lat_v[...].reshape(rows, width)
    wide = flat.astype(F32)
    factor = lax.rsqrt(jnp.mean(wide * wide, axis=-1, keepdims=True) + EPSILON)
    query = (dot(flat, wq_v[...]) * factor).astype(BF)
    qsend[...] = query.reshape(depth, lat_rows, cols)
    q_place = qbuf.at[pl.ds(pl.multiple_of(chip * lat_rows, lat_rows), lat_rows)]

    def q_copy(k):
        to = far(k)
        return remote(
            qsend.at[lax.rem(to, depth), :, column(to // depth, HD)], q_place,
            q_ssem.at[k], q_rsem.at[k], 2 * to + core, tensor,
        )

    q_own = pltpu.make_async_copy(qsend.at[place_z, :, column(upper, HD)], q_place, q_rsem.at[0])
    q_own.start()

    @pl.loop(1, chips)
    def _(k):
        q_copy(k).start()

    @pl.loop(depth, chips)
    def _(k):
        kv_copy(k, 0, keys_hbm).start()
        kv_copy(k, 1, values_hbm).start()

    for load in loads[3:]:
        load.start()

    loads[2].wait()
    latents = 2 * chips * lat_rows
    cut_row = cut_v[pl.ds(place_z, 1), :].astype(F32)
    for n in range(4):
        local = lax.broadcasted_iota(jnp.int32, (part, 1), 0) + n * part
        place = (2 * (local // lat_rows) + core) * lat_rows + local % lat_rows
        lanes = lax.broadcasted_iota(jnp.int32, (part, latents), 1)
        cut_col[n * part : (n + 1) * part, :] = jnp.sum(
            jnp.where(lanes == place, cut_row, 0.0), axis=-1, keepdims=True
        )

    step = chips // 4
    piece = step * key_rows

    def forward(n, which):
        place = kv.at[core, which, pl.ds(n * piece, piece)]
        return remote(place, place, fw_ssem.at[which, n], fw_rsem.at[which, n], sibling, tensor)

    def take(n):
        for j in range(step):
            k = n * step + j
            if k == 0:
                kv_own(0, keys_hbm).wait()
                kv_own(1, values_hbm).wait()
            else:
                kv_copy(k, 0, keys_hbm).wait_recv()
                kv_copy(k, 1, values_hbm).wait_recv()
        forward(n, 0).start()
        forward(n, 1).start()

    def places(n, of_core):
        lane = lax.broadcasted_iota(jnp.int32, (1, piece), 1)
        base = jnp.zeros((1, piece), jnp.int32)
        for j in range(step):
            start = (2 * near(n * step + j) + of_core) * key_rows
            base = jnp.where(lane // key_rows == j, start, base)
        return (base + lane % key_rows).astype(F32)

    def cross(n, at, first, last):
        query, cut = qbuf[at, :], cut_col[at, :]
        span = slice(n * piece, (n + 1) * piece)
        scores = [
            jnp.where(
                places(n, of) < cut, dot_t(query, kv[of, 0, span, :]) * SCALE, MASKED
            )
            for of in range(2)
        ]
        largest = jnp.max(jnp.maximum(scores[0], scores[1]), axis=-1, keepdims=True)
        if not first:
            before = run_max[at, :]
            largest = jnp.maximum(largest, before)
        weights = [jnp.exp2(s - largest) for s in scores]
        total = jnp.sum(weights[0] + weights[1], axis=-1, keepdims=True)
        summed = dot(weights[0].astype(BF), kv[0, 1, span, :]) + dot(
            weights[1].astype(BF), kv[1, 1, span, :]
        )
        if not first:
            fade = jnp.exp2(before - largest)
            total = total + fade * run_total[at, :]
            summed = summed + fade * run_sum[at, :]
        if last:
            return (summed / total).astype(BF)
        run_max[at, :] = largest
        run_total[at, :] = total
        run_sum[at, :] = summed

    def forwarded(n):
        forward(n, 0).wait_recv()
        forward(n, 1).wait_recv()

    take(0)
    q_own.wait()

    @pl.loop(1, chips)
    def _(k):
        q_copy(k).wait_recv()

    for n in range(1, 4):
        take(n)
        forwarded(n - 1)

        @pl.loop(0, 2)
        def _(m, n=n):
            cross(n - 1, pl.ds(pl.multiple_of(m * rows, rows), rows), n == 1, False)

    lat_place = latres.at[pl.ds(pl.multiple_of(place_z * lat_rows, lat_rows), lat_rows)]

    def lat_copy(k):
        to_seq = lax.rem(place_z + k, depth)
        return remote(
            lat_hbm.at[to_seq, :, column(tensor, cols)], lat_place,
            lat_ssem.at[k], lat_rsem.at[place_z],
            2 * (lax.rem(upper + twist, 2) * depth + to_seq) + core, tensor,
        )

    @pl.when(twist == 0)
    def _():
        pltpu.make_async_copy(
            lat_hbm.at[place_z, :, column(tensor, cols)], lat_place, lat_rsem.at[place_z]
        ).start()

    @pl.when(twist != 0)
    def _():
        lat_copy(0).start()

    @pl.loop(1, depth)
    def _(k):
        lat_copy(k).start()

    def ctx_copy(half):
        return remote(
            ctxsend.at[part_rows(half)], ctx.at[part_rows(half), column(upper, HD)],
            ctx_ssem.at[half], ctx_rsem.at[half], pair, tensor,
        )

    def y_copy(phase, half, d):
        at = part_rows(half)
        return remote(
            ysend.at[phase, d, at], yrecv.at[phase, d, at],
            rsy_ssem.at[phase, half, d], rsy_rsem.at[phase, half, d], mate_hist, mate_tensor,
        )

    def x_copy(phase, half, d):
        at = part_rows(half)
        return remote(
            xsend.at[phase, d, at], xrecv.at[phase, d, at],
            rsx_ssem.at[phase, half, d], rsx_rsem.at[phase, half, d], hist, x_peer(d),
        )

    away = [2, 1, 3] if across == 4 else list(range(1, across))

    def scatter_first(phase, half, left, weight):
        at = part_rows(half)
        for d in away + [0]:
            to = (1 - lane_y) * across + lax.rem(place_x + d, across)
            ysend[phase, d, at, :] = dot(left, weight[:, column(to, cols)]).astype(BF)
            y_copy(phase, half, d).start()
        for d in away + [0]:
            partial[d, at, :] = dot(left, weight[:, column(x_peer(d), cols)])

    def scatter_second(phase, half):
        at = part_rows(half)
        for d in away:
            y_copy(phase, half, d).wait_recv()
            xsend[phase, d, at, :] = (
                partial[d, at, :] + yrecv[phase, d, at, :].astype(F32)
            ).astype(BF)
            x_copy(phase, half, d).start()

    def scatter_last(phase, half, residual):
        at = part_rows(half)
        y_copy(phase, half, 0).wait_recv()
        total = residual.astype(F32) + partial[0, at, :] + yrecv[phase, 0, at, :].astype(F32)
        for d in away:
            x_copy(phase, half, d).wait_recv()
            total = total + xrecv[phase, d, at, :].astype(F32)
        return total.astype(BF)

    def gx_copy(phase, half, d):
        at = part_rows(half)
        return remote(
            blocks.at[phase, 0, 0, at], blocks.at[phase, 0, d, at],
            agx_ssem.at[phase, half, d], agx_rsem.at[phase, half, d], hist, x_peer(d),
        )

    def gy_copy(phase, half, d):
        at = part_rows(half)
        return remote(
            blocks.at[phase, 0, d, at], blocks.at[phase, 1, d, at],
            agy_ssem.at[phase, half, d], agy_rsem.at[phase, half, d], mate_hist, mate_tensor,
        )

    def gather_start(phase, half, block):
        blocks[phase, 0, 0, part_rows(half), :] = block
        for d in away:
            gx_copy(phase, half, d).start()
        gy_copy(phase, half, 0).start()

    def gather_forward(phase, half):
        for d in away:
            gx_copy(phase, half, d).wait_recv()
            gy_copy(phase, half, d).start()

    def gather_use(phase, half, row, weights, state):
        squares, sums = state
        for d in [0] + away:
            if row:
                gy_copy(phase, half, d).wait_recv()
            source = lax.rem(lane_y + row, 2) * across + lax.rem(place_x - d + across, across)
            block = blocks[phase, row, d, part_rows(half), :]
            wide = block.astype(F32)
            squares = squares + jnp.sum(wide * wide, axis=-1, keepdims=True)
            sums = [s + dot(block, w(column(source, cols))) for s, w in zip(sums, weights)]
        return squares, sums

    def gather_norm(state):
        squares, sums = state
        factor = lax.rsqrt(squares * (1.0 / width) + EPSILON)
        return [s * factor for s in sums]

    forwarded(3)

    def last_cross(of_half, half):
        start = pl.multiple_of(of_half * rows + half * part, part)
        return cross(3, pl.ds(start, part), False, True)

    for half in range(2):
        ctxsend[part_rows(half), :] = last_cross(1 - own_half, half)
        ctx_copy(half).start()
    loads[3].wait()
    for half in range(2):
        ctx[part_rows(half), column(upper, HD)] = last_cross(own_half, half)
    for half in range(2):
        ctx_copy(half).wait_recv()
        scatter_first(0, half, ctx[part_rows(half), :], wo_v)
    for half in range(2):
        scatter_second(0, half)
    for k in range(depth):
        lat_slot = latres.at[pl.ds(k * lat_rows, lat_rows)]
        pltpu.make_async_copy(lat_slot, lat_slot, lat_rsem.at[k]).wait()
    for half in range(2):
        gather_start(0, half, scatter_last(0, half, latres[part_rows(half), :]))

    loads[4].wait()
    qkv_weights = [lambda at, n=n: wqkv_v[n, at, :] for n in range(3)]

    def kvs_copy(which, half, source, slot, device):
        at = part_rows(half)
        return remote(
            kvs.at[source, which, at], kvs.at[slot, which, at],
            kvs_ssem.at[which, half, slot], kvs_rsem.at[which, half, slot], device, tensor,
        )

    def project_self(half, state):
        self_q, self_k, self_v = gather_norm(state)
        at = part_rows(half)
        kvs[0, 0, at, :] = self_k.astype(BF)
        kvs[0, 1, at, :] = self_v.astype(BF)
        for which in range(2):
            kvs_copy(which, half, 0, 2, pair).start()
        for which in range(2):
            kvs_copy(which, half, 0, 1, sibling).start()
        qself[at, :] = self_q.astype(BF)

    def empty(weights):
        return 0.0, [0.0 for _ in weights]

    gather_forward(0, 0)
    state = gather_use(0, 0, 0, qkv_weights, empty(qkv_weights))
    gather_forward(0, 1)
    project_self(0, gather_use(0, 0, 1, qkv_weights, state))
    state = gather_use(0, 1, 0, qkv_weights, empty(qkv_weights))
    project_self(1, gather_use(0, 1, 1, qkv_weights, state))
    for half in range(2):
        for which in range(2):
            kvs_copy(which, half, 0, 2, pair).wait_recv()
            kvs_copy(which, half, 2, 3, sibling).start()
    for half in range(2):
        for which in range(2):
            kvs_copy(which, half, 0, 1, sibling).wait_recv()
            kvs_copy(which, half, 2, 3, sibling).wait_recv()

    def latent_place(local, of_half, of_core):
        return (2 * (of_half * depth + local // lat_rows) + of_core) * lat_rows + local % lat_rows

    holders = [
        (own_half, core), (sibling_half, other_core),
        (1 - own_half, core), (1 - sibling_half, other_core),
    ]
    loads[5].wait()
    for half in range(2):
        own_place = latent_place(
            lax.broadcasted_iota(jnp.int32, (part, 1), 0) + half * part, own_half, core
        )
        lane = lax.broadcasted_iota(jnp.int32, (1, rows), 1)
        for h in range(cols // HD):
            at = slice(h * HD, (h + 1) * HD)
            mixed[part_rows(half), at] = attend(
                qself[part_rows(half), at],
                [
                    (kvs[slot, 0, :, at], kvs[slot, 1, :, at], latent_place(lane, *held) <= own_place)
                    for slot, held in enumerate(holders)
                ],
            )
        scatter_first(1, half, mixed[part_rows(half), :], wos_v)
    for half in range(2):
        scatter_second(1, half)
    for half in range(2):
        gather_start(
            1, half, scatter_last(1, half, blocks[0, 0, 0, part_rows(half), :])
        )
    loads[6].wait()
    loads[7].wait()
    up_weights = [lambda at: wup_v[at, :]]

    def mlp(half, state):
        (raised,) = gather_norm(state)
        scatter_first(2, half, jax.nn.gelu(raised).astype(BF), wdn_v)

    gather_forward(1, 0)
    state = gather_use(1, 0, 0, up_weights, empty(up_weights))
    gather_forward(1, 1)
    mlp(0, gather_use(1, 0, 1, up_weights, state))
    state = gather_use(1, 1, 0, up_weights, empty(up_weights))
    mlp(1, gather_use(1, 1, 1, up_weights, state))
    for half in range(2):
        scatter_second(2, half)

    def out_copy(n):
        return remote(
            enc.at[pl.ds(pl.multiple_of(n * lat_rows, lat_rows), lat_rows)],
            out_hbm.at[place_z], out_ssem.at[n], out_rsem.at[place_z],
            2 * (own_half * depth + n) + core, tensor,
        )

    def elsewhere(n):
        return jnp.logical_or(n != place_z, twist != 0)

    for half in range(2):
        enc[part_rows(half), :] = scatter_last(2, half, blocks[1, 0, 0, part_rows(half), :])

        @pl.loop(half * (depth // 2), (half + 1) * (depth // 2))
        def _(n):
            @pl.when(elsewhere(n))
            def _():
                out_copy(n).start()

    @pl.when(twist == 0)
    def _():
        pltpu.make_async_copy(
            enc.at[pl.ds(pl.multiple_of(place_z * lat_rows, lat_rows), lat_rows)],
            out_hbm.at[place_z], out_rsem.at[place_z],
        ).start()

    @pl.loop(1, chips)
    def _(k):
        kv_copy(k, 0, keys_hbm).wait_send()
        kv_copy(k, 1, values_hbm).wait_send()
        q_copy(k).wait_send()

    @pl.when(twist != 0)
    def _():
        lat_copy(0).wait_send()

    @pl.loop(1, depth)
    def _(k):
        lat_copy(k).wait_send()

    for n in range(4):
        forward(n, 0).wait_send()
        forward(n, 1).wait_send()
    for half in range(2):
        ctx_copy(half).wait_send()
        for phase in range(3):
            for d in range(across):
                y_copy(phase, half, d).wait_send()
            for d in away:
                x_copy(phase, half, d).wait_send()
        for phase in range(2):
            for d in range(across):
                gy_copy(phase, half, d).wait_send()
            for d in away:
                gx_copy(phase, half, d).wait_send()
        for which in range(2):
            kvs_copy(which, half, 0, 2, pair).wait_send()
            kvs_copy(which, half, 0, 1, sibling).wait_send()
            kvs_copy(which, half, 2, 3, sibling).wait_send()

    for n in range(depth):
        pltpu.make_async_copy(out_hbm.at[n], out_hbm.at[n], out_rsem.at[n]).wait()

    @pl.loop(0, depth)
    def _(n):
        @pl.when(elsewhere(n))
        def _():
            out_copy(n).wait_send()


def body(latents, keys, values, cutoff, w_q, w_o, w_qkv, w_os, w_up, w_down):
    seqs, lat_rows, width = latents.shape
    key_rows, cols = keys.shape[1:]
    chips = lax.axis_size("hist") // 2
    tensors = lax.axis_size("tensor")
    across = tensors // 2
    depth = chips // 2
    rows = seqs * lat_rows

    def vmem(*shape):
        return pltpu.VMEM(shape, BF)

    def wide(*shape):
        return pltpu.VMEM(shape, F32)

    dma = pltpu.SemaphoreType.DMA
    hbm = pl.BlockSpec(memory_space=pltpu.HBM)
    return pl.pallas_call(
        functools.partial(step_kernel, (chips, tensors, lat_rows, key_rows, width)),
        out_shape=jax.ShapeDtypeStruct((seqs, lat_rows, cols), BF),
        in_specs=[hbm] * 10,
        out_specs=hbm,
        scratch_shapes=[
            vmem(*latents.shape), pltpu.VMEM(cutoff.shape, jnp.int32),
            vmem(*w_q.shape), vmem(*w_o.shape), vmem(*w_qkv.shape),
            vmem(*w_os.shape), vmem(*w_up.shape), vmem(*w_down.shape),
            vmem(2, 2, chips * key_rows, HD),
            vmem(seqs, lat_rows, cols),
            vmem(chips * lat_rows, HD),
            wide(chips * lat_rows, 1), wide(chips * lat_rows, 1), wide(chips * lat_rows, 1),
            wide(chips * lat_rows, HD),
            vmem(rows, cols),
            vmem(rows, HD),
            vmem(rows, cols),
            wide(across, rows, cols),
            vmem(3, across, rows, cols), vmem(3, across, rows, cols),
            vmem(3, across, rows, cols), vmem(3, across, rows, cols),
            vmem(2, 2, across, rows, cols),
            vmem(rows, cols),
            vmem(4, 2, rows, cols),
            vmem(rows, cols),
            vmem(rows, cols),
            dma((8,)),
            dma((2, chips)), dma((2, chips)),
            dma((2, 4)), dma((2, 4)),
            dma((chips,)), dma((chips,)),
            dma((depth,)), dma((depth,)),
            dma((2,)), dma((2,)),
            dma((3, 2, across)), dma((3, 2, across)), dma((3, 2, across)), dma((3, 2, across)),
            dma((2, 2, across)), dma((2, 2, across)), dma((2, 2, across)), dma((2, 2, across)),
            dma((2, 2, 4)), dma((2, 2, 4)),
            dma((depth,)), dma((depth,)),
        ],
        compiler_params=pltpu.CompilerParams(
            collective_id=0, has_side_effects=True, vmem_limit_bytes=60 * 1024 * 1024
        ),
        cost_estimate=pl.CostEstimate(
            flops=8 * rows * width * cols * 5, bytes_accessed=12 * 1024 * 1024, transcendentals=0
        ),
    )(latents, keys, values, cutoff, w_q, w_o, w_qkv, w_os, w_up, w_down)


def solution(mesh):
    placed = (
        P(None, "hist", None),
        P(None, "hist", "tensor"),
        P(None, "hist", "tensor"),
        P(),
        P(None, "tensor"),
        P("tensor", None),
        P(None, None, "tensor"),
        P("tensor", None),
        P(None, "tensor"),
        P("tensor", None),
    )
    return jax.shard_map(
        body, mesh=mesh, in_specs=placed, out_specs=P(None, "hist", "tensor"), check_vma=False
    )
```

```python
import functools
import math

import jax
import jax.numpy as jnp
from jax import lax
from jax.experimental import pallas as pl
from jax.experimental.pallas import tpu as pltpu
from jax.sharding import PartitionSpec as P

HD = 128
EPSILON = 1e-06
MASKED = -1e30
MESH = pl.DeviceIdType.MESH
BF = jnp.bfloat16
F32 = jnp.float32
PARTS = 4
LAG = 0.67
SCALE = math.log2(math.e) / math.sqrt(HD)


def dot(left, right):
    return jnp.dot(left, right, preferred_element_type=F32)


def dot_t(left, right):
    return lax.dot_general(left, right, (((1,), (1,)), ((), ())), preferred_element_type=F32)


def remote(src, dst, send_sem, recv_sem, hist, tensor):
    return pltpu.make_async_remote_copy(
        src_ref=src,
        dst_ref=dst,
        send_sem=send_sem,
        recv_sem=recv_sem,
        device_id=(hist, tensor),
        device_id_type=MESH,
    )


def attend(query, pieces):
    scores = [jnp.where(seen, dot_t(query, keys) * SCALE, MASKED) for keys, _, seen in pieces]
    largest = functools.reduce(jnp.maximum, [jnp.max(s, axis=-1, keepdims=True) for s in scores])
    total = jnp.zeros_like(largest)
    summed = jnp.zeros((query.shape[0], HD), F32)
    for score, (_, values, _) in zip(scores, pieces):
        weights = jnp.exp2(score - largest)
        total = total + jnp.sum(weights, axis=-1, keepdims=True)
        summed = summed + dot(weights.astype(BF), values)
    return (summed / total).astype(BF)


def step_kernel(
    sizes,
    lat_hbm, keys_hbm, values_hbm, cut_hbm, wq_hbm, wo_hbm, wqkv_hbm, wos_hbm, wup_hbm, wdn_hbm,
    out_hbm,
    lat_v, cut_v, wq_v, wo_v, wqkv_v, wos_v, wup_v, wdn_v,
    kv, qsend, qbuf, cut_col, run_max, run_total, run_sum, latres, ctxsend, ctx,
    partial, ysend, yrecv, xsend, xrecv, blocks, qself, kvs, mixed, enc,
    load_sem, kv_ssem, kv_rsem, fw_ssem, fw_rsem, q_ssem, q_rsem, lat_ssem, lat_rsem,
    ctx_ssem, ctx_rsem, rsy_ssem, rsy_rsem, rsx_ssem, rsx_rsem, agy_ssem, agy_rsem, agx_ssem, agx_rsem,
    kvs_ssem, kvs_rsem, out_ssem, out_rsem,
):
    chips, tensors, lat_rows, key_rows, width = sizes
    depth = chips // 2
    rows = depth * lat_rows
    part = rows // PARTS
    block_rows = rows // 2
    cols = width // tensors
    across = tensors // 2
    hist = lax.axis_index("hist")
    tensor = lax.axis_index("tensor")
    core = lax.rem(hist, 2)
    chip = hist // 2
    upper = chip // depth
    place_z = lax.rem(chip, depth)
    lane_y = tensor // across
    place_x = lax.rem(tensor, across)
    other_core = 1 - core
    sibling = 2 * chip + other_core
    pair = 2 * ((1 - upper) * depth + place_z) + core
    twist = core * lane_y
    own_half = lax.rem(upper + twist, 2)
    sibling_half = lax.rem(upper + other_core * lane_y, 2)
    parity = lax.rem(chip, 2)
    holder = lax.rem(parity + twist, 2)
    slot = chip // 2
    mate_hist = 2 * (lax.rem(upper + core, 2) * depth + place_z) + core
    mate_tensor = (1 - lane_y) * across + place_x

    def column(index, size):
        return pl.ds(pl.multiple_of(index * size, size), size)

    def part_rows(half):
        return pl.ds(half * part, part)

    def x_peer(d):
        return lane_y * across + lax.rem(place_x + d, across)

    def far(k):
        j = k // 2
        dz = ((j + 1) // 2) * (2 * (j % 2) - 1)
        return lax.rem(upper + k % 2, 2) * depth + lax.rem(place_z + depth + dz, depth)

    def near(k):
        j = k // 2
        dz = ((j + 1) // 2) * (2 * (j % 2) - 1)
        return lax.rem(upper + k % 2, 2) * depth + lax.rem(place_z + depth - dz, depth)

    loads = [
        pltpu.make_async_copy(src, dst, load_sem.at[n])
        for n, (src, dst) in enumerate(
            [(lat_hbm, lat_v), (wq_hbm, wq_v), (cut_hbm, cut_v), (wo_hbm, wo_v), (wqkv_hbm, wqkv_v),
             (wos_hbm, wos_v), (wup_hbm, wup_v), (wdn_hbm, wdn_v)]
        )
    ]
    for load in loads[:3]:
        load.start()

    barrier = pltpu.get_barrier_semaphore()

    @pl.loop(1, chips)
    def _(k):
        pl.semaphore_signal(
            barrier, inc=1, device_id=(2 * near(k) + core, tensor), device_id_type=MESH
        )

    for d in range(1, across):
        pl.semaphore_signal(barrier, inc=1, device_id=(hist, x_peer(d)), device_id_type=MESH)
    pl.semaphore_signal(barrier, inc=1, device_id=(mate_hist, mate_tensor), device_id_type=MESH)
    pl.semaphore_signal(barrier, inc=1, device_id=(sibling, tensor), device_id_type=MESH)
    pl.semaphore_wait(barrier, chips - 1 + across - 1 + 2)

    def kv_copy(k, which, array):
        to = far(k)
        return remote(
            array.at[lax.rem(to, depth), :, column(to // depth, HD)],
            kv.at[core, which, pl.ds(pl.multiple_of(k * key_rows, key_rows), key_rows)],
            kv_ssem.at[which, k], kv_rsem.at[which, k], 2 * to + core, tensor,
        )

    def kv_own(which, array):
        return pltpu.make_async_copy(
            array.at[place_z, :, column(upper, HD)],
            kv.at[core, which, pl.ds(0, key_rows)],
            kv_rsem.at[which, 0],
        )

    kv_own(0, keys_hbm).start()
    kv_own(1, values_hbm).start()

    @pl.loop(1, depth)
    def _(k):
        kv_copy(k, 0, keys_hbm).start()
        kv_copy(k, 1, values_hbm).start()

    loads[0].wait()
    loads[1].wait()
    flat = lat_v[...].reshape(rows, width)
    wide = flat.astype(F32)
    factor = lax.rsqrt(jnp.mean(wide * wide, axis=-1, keepdims=True) + EPSILON)
    query = (dot(flat, wq_v[...]) * factor).astype(BF)
    qsend[...] = query.reshape(depth, lat_rows, cols)
    q_place = qbuf.at[
        pl.ds(pl.multiple_of((parity * depth + slot) * lat_rows, lat_rows), lat_rows)
    ]

    def q_copy(k):
        to = far(k)
        return remote(
            qsend.at[lax.rem(to, depth), :, column(to // depth, HD)], q_place,
            q_ssem.at[k], q_rsem.at[k], 2 * to + core, tensor,
        )

    q_own = pltpu.make_async_copy(qsend.at[place_z, :, column(upper, HD)], q_place, q_rsem.at[0])
    q_own.start()

    @pl.loop(1, chips)
    def _(k):
        q_copy(k).start()

    @pl.loop(depth, chips)
    def _(k):
        kv_copy(k, 0, keys_hbm).start()
        kv_copy(k, 1, values_hbm).start()

    for load in loads[3:]:
        load.start()

    def latent_place(row, of_half, of_core):
        return (2 * (2 * (row // lat_rows) + of_half) + of_core) * lat_rows + row % lat_rows

    loads[2].wait()
    latents = 2 * chips * lat_rows
    cut_row = cut_v[pl.ds(place_z, 1), :].astype(F32)
    for n in range(4):
        local = lax.broadcasted_iota(jnp.int32, (block_rows, 1), 0) + n % 2 * block_rows
        place = latent_place(local, n // 2, core)
        lanes = lax.broadcasted_iota(jnp.int32, (block_rows, latents), 1)
        cut_col[n * block_rows : (n + 1) * block_rows, :] = jnp.sum(
            jnp.where(lanes == place, cut_row, 0.0), axis=-1, keepdims=True
        )

    step = chips // 4
    piece = step * key_rows

    def forward(n, which):
        place = kv.at[core, which, pl.ds(n * piece, piece)]
        return remote(place, place, fw_ssem.at[which, n], fw_rsem.at[which, n], sibling, tensor)

    def take(n):
        for j in range(step):
            k = n * step + j
            if k == 0:
                kv_own(0, keys_hbm).wait()
                kv_own(1, values_hbm).wait()
            else:
                kv_copy(k, 0, keys_hbm).wait_recv()
                kv_copy(k, 1, values_hbm).wait_recv()
        forward(n, 0).start()
        forward(n, 1).start()

    def places(n, of_core):
        lane = lax.broadcasted_iota(jnp.int32, (1, piece), 1)
        base = jnp.zeros((1, piece), jnp.int32)
        for j in range(step):
            start = (2 * near(n * step + j) + of_core) * key_rows
            base = jnp.where(lane // key_rows == j, start, base)
        return (base + lane % key_rows).astype(F32)

    def cross(n, at, first, last):
        query, cut = qbuf[at, :], cut_col[at, :]
        span = slice(n * piece, (n + 1) * piece)
        scores = [
            jnp.where(
                places(n, of) < cut, dot_t(query, kv[of, 0, span, :]) * SCALE, MASKED
            )
            for of in range(2)
        ]
        largest = jnp.max(jnp.maximum(scores[0], scores[1]), axis=-1, keepdims=True)
        if not first:
            before = run_max[at, :]
            largest = jnp.maximum(largest, before)
        weights = [jnp.exp2(s - largest) for s in scores]
        total = jnp.sum(weights[0] + weights[1], axis=-1, keepdims=True)
        summed = dot(weights[0].astype(BF), kv[0, 1, span, :]) + dot(
            weights[1].astype(BF), kv[1, 1, span, :]
        )
        if not first:
            fade = jnp.exp2(before - largest)
            total = total + fade * run_total[at, :]
            summed = summed + fade * run_sum[at, :]
        if last:
            return (summed / total).astype(BF)
        run_max[at, :] = largest
        run_total[at, :] = total
        run_sum[at, :] = summed

    def forwarded(n):
        forward(n, 0).wait_recv()
        forward(n, 1).wait_recv()

    take(0)
    q_own.wait()

    @pl.loop(1, chips)
    def _(k):
        q_copy(k).wait_recv()

    for n in range(1, 4):
        take(n)
        forwarded(n - 1)

        @pl.loop(0, 2)
        def _(m, n=n):
            cross(n - 1, pl.ds(pl.multiple_of(m * rows, rows), rows), n == 1, False)

    lat_place = latres.at[pl.ds(pl.multiple_of(slot * lat_rows, lat_rows), lat_rows)]

    def lat_copy(k):
        to_seq = lax.rem(place_z + k, depth)
        return remote(
            lat_hbm.at[to_seq, :, column(tensor, cols)], lat_place,
            lat_ssem.at[k], lat_rsem.at[slot],
            2 * (holder * depth + to_seq) + core, tensor,
        )

    @pl.when(holder == upper)
    def _():
        pltpu.make_async_copy(
            lat_hbm.at[place_z, :, column(tensor, cols)], lat_place, lat_rsem.at[slot]
        ).start()

    @pl.when(holder != upper)
    def _():
        lat_copy(0).start()

    @pl.loop(1, depth)
    def _(k):
        lat_copy(k).start()

    def block_at(half):
        return pl.ds(half * block_rows, block_rows)

    def ctx_copy(half):
        return remote(
            ctxsend.at[block_at(half)], ctx.at[block_at(half), column(upper, HD)],
            ctx_ssem.at[half], ctx_rsem.at[half], pair, tensor,
        )

    def y_copy(phase, half, d):
        at = part_rows(half)
        return remote(
            ysend.at[phase, d, at], yrecv.at[phase, d, at],
            rsy_ssem.at[phase, half, d], rsy_rsem.at[phase, half, d], mate_hist, mate_tensor,
        )

    def x_copy(phase, half, d):
        at = part_rows(half)
        return remote(
            xsend.at[phase, d, at], xrecv.at[phase, d, at],
            rsx_ssem.at[phase, half, d], rsx_rsem.at[phase, half, d], hist, x_peer(d),
        )

    away = [2, 1, 3] if across == 4 else list(range(1, across))

    def scatter_first(phase, half, left, weight):
        at = part_rows(half)
        for d in away + [0]:
            to = (1 - lane_y) * across + lax.rem(place_x + d, across)
            ysend[phase, d, at, :] = dot(left, weight[:, column(to, cols)]).astype(BF)
            y_copy(phase, half, d).start()
        for d in away + [0]:
            partial[d, at, :] = dot(left, weight[:, column(x_peer(d), cols)])

    def scatter_second(phase, half):
        at = part_rows(half)
        for d in away:
            y_copy(phase, half, d).wait_recv()
            xsend[phase, d, at, :] = (
                partial[d, at, :] + yrecv[phase, d, at, :].astype(F32)
            ).astype(BF)
            x_copy(phase, half, d).start()

    def scatter_last(phase, half, residual):
        at = part_rows(half)
        y_copy(phase, half, 0).wait_recv()
        total = residual.astype(F32) + partial[0, at, :] + yrecv[phase, 0, at, :].astype(F32)
        for d in away:
            x_copy(phase, half, d).wait_recv()
            total = total + xrecv[phase, d, at, :].astype(F32)
        return total.astype(BF)

    def gx_copy(phase, half, d):
        at = part_rows(half)
        return remote(
            blocks.at[phase, 0, 0, at], blocks.at[phase, 0, d, at],
            agx_ssem.at[phase, half, d], agx_rsem.at[phase, half, d], hist, x_peer(d),
        )

    def gy_copy(phase, half, d):
        at = part_rows(half)
        return remote(
            blocks.at[phase, 0, d, at], blocks.at[phase, 1, d, at],
            agy_ssem.at[phase, half, d], agy_rsem.at[phase, half, d], mate_hist, mate_tensor,
        )

    def gather_start(phase, half, block):
        blocks[phase, 0, 0, part_rows(half), :] = block
        for d in away:
            gx_copy(phase, half, d).start()
        gy_copy(phase, half, 0).start()

    def gather_forward(phase, half):
        for d in away:
            gx_copy(phase, half, d).wait_recv()
            gy_copy(phase, half, d).start()

    def gather_use(phase, half, row, weights, state):
        squares, sums = state
        for d in [0] + away:
            if row:
                gy_copy(phase, half, d).wait_recv()
            source = lax.rem(lane_y + row, 2) * across + lax.rem(place_x - d + across, across)
            block = blocks[phase, row, d, part_rows(half), :]
            wide = block.astype(F32)
            squares = squares + jnp.sum(wide * wide, axis=-1, keepdims=True)
            sums = [s + dot(block, w(column(source, cols))) for s, w in zip(sums, weights)]
        return squares, sums

    def gather_norm(state):
        squares, sums = state
        factor = lax.rsqrt(squares * (1.0 / width) + EPSILON)
        return [s * factor for s in sums]

    forwarded(3)

    def last_cross(of_half, half):
        start = pl.multiple_of(of_half * rows + half * block_rows, block_rows)
        return cross(3, pl.ds(start, block_rows), False, True)

    for half in range(2):
        ctxsend[block_at(half), :] = last_cross(1 - own_half, half)
        ctx_copy(half).start()
    for half in range(2):
        ctx[block_at(half), column(upper, HD)] = last_cross(own_half, half)
    for load in loads[3:]:
        load.wait()

    def kvs_rows(p, holder_slot):
        return pl.ds((p * 4 + holder_slot) * part, part)

    def kvs_copy(which, p, source, target, device):
        return remote(
            kvs.at[which, kvs_rows(p, source)], kvs.at[which, kvs_rows(p, target)],
            kvs_ssem.at[which, p, target], kvs_rsem.at[which, p, target], device, tensor,
        )

    holders = [
        (own_half, core), (sibling_half, other_core),
        (1 - own_half, core), (1 - sibling_half, other_core),
    ]
    qkv_weights = [lambda at, n=n: wqkv_v[n, at, :] for n in range(3)]
    up_weights = [lambda at: wup_v[at, :]]
    states = {}

    def out_copy(n):
        return remote(
            enc.at[pl.ds(pl.multiple_of(n * lat_rows, lat_rows), lat_rows)],
            out_hbm.at[place_z], out_ssem.at[n], out_rsem.at[place_z],
            2 * (2 * n + own_half) + core, tensor,
        )

    def elsewhere(n):
        return 2 * n + own_half != chip

    def project_context(p):
        if p % (PARTS // 2) == 0:
            ctx_copy(p // (PARTS // 2)).wait_recv()
        scatter_first(0, p, ctx[part_rows(p), :], wo_v)

    def add_latents(p):
        for k in range(p * depth // PARTS, (p + 1) * depth // PARTS):
            lat_slot = latres.at[pl.ds(k * lat_rows, lat_rows)]
            pltpu.make_async_copy(lat_slot, lat_slot, lat_rsem.at[k]).wait()
        gather_start(0, p, scatter_last(0, p, latres[part_rows(p), :]))

    def gather_near(phase, p, weights):
        gather_forward(phase, p)
        states[phase, p] = gather_use(phase, p, 0, weights, (0.0, [0.0 for _ in weights]))

    def project_self(p):
        self_q, self_k, self_v = gather_norm(gather_use(0, p, 1, qkv_weights, states[0, p]))
        kvs[0, kvs_rows(p, 0), :] = self_k.astype(BF)
        kvs[1, kvs_rows(p, 0), :] = self_v.astype(BF)
        for which in range(2):
            kvs_copy(which, p, 0, 2, pair).start()
        for which in range(2):
            kvs_copy(which, p, 0, 1, sibling).start()
        qself[part_rows(p), :] = self_q.astype(BF)

    def share(p):
        for which in range(2):
            kvs_copy(which, p, 0, 2, pair).wait_recv()
            kvs_copy(which, p, 2, 3, sibling).start()

    def attend_self(p):
        for which in range(2):
            kvs_copy(which, p, 0, 1, sibling).wait_recv()
            kvs_copy(which, p, 2, 3, sibling).wait_recv()
        own_place = latent_place(
            lax.broadcasted_iota(jnp.int32, (part, 1), 0) + p * part, own_half, core
        )
        seen = (p + 1) * 4 * part
        lane = lax.broadcasted_iota(jnp.int32, (1, seen), 1)
        by = lane // part % 4
        row = lane // (4 * part) * part + lane % part
        place = latent_place(row, *holders[0])
        for n in range(1, 4):
            place = jnp.where(by == n, latent_place(row, *holders[n]), place)
        visible = place <= own_place
        for h in range(cols // HD):
            at = slice(h * HD, (h + 1) * HD)
            mixed[part_rows(p), at] = attend(
                qself[part_rows(p), at], [(kvs[0, :seen, at], kvs[1, :seen, at], visible)]
            )
        scatter_first(1, p, mixed[part_rows(p), :], wos_v)

    def add_first(p):
        gather_start(1, p, scatter_last(1, p, blocks[0, 0, 0, part_rows(p), :]))

    def mlp(p):
        (raised,) = gather_norm(gather_use(1, p, 1, up_weights, states[1, p]))
        scatter_first(2, p, jax.nn.gelu(raised).astype(BF), wdn_v)

    def send_back(p):
        enc[part_rows(p), :] = scatter_last(2, p, blocks[1, 0, 0, part_rows(p), :])

        @pl.loop(p * depth // PARTS, (p + 1) * depth // PARTS)
        def _(n):
            @pl.when(elsewhere(n))
            def _():
                out_copy(n).start()

    steps = [
        project_context,
        lambda p: scatter_second(0, p),
        add_latents,
        lambda p: gather_near(0, p, qkv_weights),
        project_self,
        share,
        attend_self,
        lambda p: scatter_second(1, p),
        add_first,
        lambda p: gather_near(1, p, up_weights),
        mlp,
        lambda p: scatter_second(2, p),
        send_back,
    ]
    for _, p, n in sorted((n + LAG * p, p, n) for n in range(len(steps)) for p in range(PARTS)):
        steps[n](p)

    @pl.when(parity == own_half)
    def _():
        pltpu.make_async_copy(
            enc.at[pl.ds(pl.multiple_of(slot * lat_rows, lat_rows), lat_rows)],
            out_hbm.at[place_z], out_rsem.at[place_z],
        ).start()

    @pl.loop(1, chips)
    def _(k):
        kv_copy(k, 0, keys_hbm).wait_send()
        kv_copy(k, 1, values_hbm).wait_send()
        q_copy(k).wait_send()

    @pl.when(holder != upper)
    def _():
        lat_copy(0).wait_send()

    @pl.loop(1, depth)
    def _(k):
        lat_copy(k).wait_send()

    for n in range(4):
        forward(n, 0).wait_send()
        forward(n, 1).wait_send()
    for half in range(2):
        ctx_copy(half).wait_send()
    for half in range(PARTS):
        for phase in range(3):
            for d in range(across):
                y_copy(phase, half, d).wait_send()
            for d in away:
                x_copy(phase, half, d).wait_send()
        for phase in range(2):
            for d in range(across):
                gy_copy(phase, half, d).wait_send()
            for d in away:
                gx_copy(phase, half, d).wait_send()
        for which in range(2):
            kvs_copy(which, half, 0, 2, pair).wait_send()
            kvs_copy(which, half, 0, 1, sibling).wait_send()
            kvs_copy(which, half, 2, 3, sibling).wait_send()

    for n in range(depth):
        pltpu.make_async_copy(out_hbm.at[n], out_hbm.at[n], out_rsem.at[n]).wait()

    @pl.loop(0, depth)
    def _(n):
        @pl.when(elsewhere(n))
        def _():
            out_copy(n).wait_send()


def body(latents, keys, values, cutoff, w_q, w_o, w_qkv, w_os, w_up, w_down):
    seqs, lat_rows, width = latents.shape
    key_rows, cols = keys.shape[1:]
    chips = lax.axis_size("hist") // 2
    tensors = lax.axis_size("tensor")
    across = tensors // 2
    depth = chips // 2
    rows = seqs * lat_rows

    def vmem(*shape):
        return pltpu.VMEM(shape, BF)

    def wide(*shape):
        return pltpu.VMEM(shape, F32)

    dma = pltpu.SemaphoreType.DMA
    hbm = pl.BlockSpec(memory_space=pltpu.HBM)
    return pl.pallas_call(
        functools.partial(step_kernel, (chips, tensors, lat_rows, key_rows, width)),
        out_shape=jax.ShapeDtypeStruct((seqs, lat_rows, cols), BF),
        in_specs=[hbm] * 10,
        out_specs=hbm,
        scratch_shapes=[
            vmem(*latents.shape), pltpu.VMEM(cutoff.shape, jnp.int32),
            vmem(*w_q.shape), vmem(*w_o.shape), vmem(*w_qkv.shape),
            vmem(*w_os.shape), vmem(*w_up.shape), vmem(*w_down.shape),
            vmem(2, 2, chips * key_rows, HD),
            vmem(seqs, lat_rows, cols),
            vmem(chips * lat_rows, HD),
            wide(chips * lat_rows, 1), wide(chips * lat_rows, 1), wide(chips * lat_rows, 1),
            wide(chips * lat_rows, HD),
            vmem(rows, cols),
            vmem(rows, HD),
            vmem(rows, cols),
            wide(across, rows, cols),
            vmem(3, across, rows, cols), vmem(3, across, rows, cols),
            vmem(3, across, rows, cols), vmem(3, across, rows, cols),
            vmem(2, 2, across, rows, cols),
            vmem(rows, cols),
            vmem(2, 4 * rows, cols),
            vmem(rows, cols),
            vmem(rows, cols),
            dma((8,)),
            dma((2, chips)), dma((2, chips)),
            dma((2, 4)), dma((2, 4)),
            dma((chips,)), dma((chips,)),
            dma((depth,)), dma((depth,)),
            dma((2,)), dma((2,)),
            *[dma((3, PARTS, across))] * 4,
            *[dma((2, PARTS, across))] * 4,
            *[dma((2, PARTS, 4))] * 2,
            dma((depth,)), dma((depth,)),
        ],
        compiler_params=pltpu.CompilerParams(
            collective_id=0, has_side_effects=True, vmem_limit_bytes=60 * 1024 * 1024
        ),
        cost_estimate=pl.CostEstimate(
            flops=8 * rows * width * cols * 5, bytes_accessed=12 * 1024 * 1024, transcendentals=0
        ),
    )(latents, keys, values, cutoff, w_q, w_o, w_qkv, w_os, w_up, w_down)


def solution(mesh):
    placed = (
        P(None, "hist", None),
        P(None, "hist", "tensor"),
        P(None, "hist", "tensor"),
        P(),
        P(None, "tensor"),
        P("tensor", None),
        P(None, None, "tensor"),
        P("tensor", None),
        P(None, "tensor"),
        P("tensor", None),
    )
    return jax.shard_map(
        body, mesh=mesh, in_specs=placed, out_specs=P(None, "hist", "tensor"), check_vma=False
    )
```

```python
import functools
import math

import jax
import jax.numpy as jnp
from jax import lax
from jax.experimental import pallas as pl
from jax.experimental.pallas import tpu as pltpu
from jax.sharding import PartitionSpec as P

HD = 128
EPSILON = 1e-06
MASKED = -1e30
MESH = pl.DeviceIdType.MESH
BF = jnp.bfloat16
F32 = jnp.float32
PARTS = 4
LAG = 0.67
SCALE = math.log2(math.e) / math.sqrt(HD)


def dot(left, right):
    return jnp.dot(left, right, preferred_element_type=F32)


def dot_t(left, right):
    return lax.dot_general(left, right, (((1,), (1,)), ((), ())), preferred_element_type=F32)


def remote(src, dst, send_sem, recv_sem, hist, tensor):
    return pltpu.make_async_remote_copy(
        src_ref=src,
        dst_ref=dst,
        send_sem=send_sem,
        recv_sem=recv_sem,
        device_id=(hist, tensor),
        device_id_type=MESH,
    )


def attend(query, pieces):
    scores = [jnp.where(seen, dot_t(query, keys), MASKED) for keys, _, seen in pieces]
    largest = functools.reduce(jnp.maximum, [jnp.max(s, axis=-1, keepdims=True) for s in scores])
    total = jnp.zeros_like(largest)
    summed = jnp.zeros((query.shape[0], HD), F32)
    for score, (_, values, _) in zip(scores, pieces):
        weights = jnp.exp2(score - largest)
        total = total + jnp.sum(weights, axis=-1, keepdims=True)
        summed = summed + dot(weights.astype(BF), values)
    return (summed / total).astype(BF)


def step_kernel(
    sizes,
    lat_hbm, keys_hbm, values_hbm, cut_hbm, wq_hbm, wo_hbm, wqkv_hbm, wos_hbm, wup_hbm, wdn_hbm,
    out_hbm,
    keys_v, values_v, lat_v, cut_v, wq_v, wo_v, wqkv_v, wos_v, wup_v, wdn_v,
    kv, qsend, qbuf, cut_col, run_max, run_total, run_sum, latres, ctxsend, ctx,
    partial, ysend, yrecv, xsend, xrecv, blocks, qself, kvs, mixed, enc,
    load_sem, kv_ssem, kv_rsem, fw_ssem, fw_rsem, q_ssem, q_rsem, lat_ssem, lat_rsem,
    ctx_ssem, ctx_rsem, rsy_ssem, rsy_rsem, rsx_ssem, rsx_rsem, agy_ssem, agy_rsem, agx_ssem, agx_rsem,
    kvs_ssem, kvs_rsem, out_ssem, out_rsem,
):
    chips, tensors, lat_rows, key_rows, width = sizes
    depth = chips // 2
    rows = depth * lat_rows
    part = rows // PARTS
    block_rows = rows // 2
    cols = width // tensors
    across = tensors // 2
    hist = lax.axis_index("hist")
    tensor = lax.axis_index("tensor")
    core = lax.rem(hist, 2)
    chip = hist // 2
    upper = chip // depth
    place_z = lax.rem(chip, depth)
    lane_y = tensor // across
    place_x = lax.rem(tensor, across)
    other_core = 1 - core
    sibling = 2 * chip + other_core
    pair = 2 * ((1 - upper) * depth + place_z) + core
    twist = core * lane_y
    own_half = lax.rem(upper + twist, 2)
    sibling_half = lax.rem(upper + other_core * lane_y, 2)
    parity = lax.rem(chip, 2)
    holder = lax.rem(parity + twist, 2)
    slot = chip // 2
    mate_hist = 2 * (lax.rem(upper + core, 2) * depth + place_z) + core
    mate_tensor = (1 - lane_y) * across + place_x

    def column(index, size):
        return pl.ds(pl.multiple_of(index * size, size), size)

    def part_rows(half):
        return pl.ds(half * part, part)

    def x_peer(d):
        return lane_y * across + lax.rem(place_x + d, across)

    def far(k):
        j = k // 2
        dz = ((j + 1) // 2) * (2 * (j % 2) - 1)
        return lax.rem(upper + k % 2, 2) * depth + lax.rem(place_z + depth + dz, depth)

    def near(k):
        j = k // 2
        dz = ((j + 1) // 2) * (2 * (j % 2) - 1)
        return lax.rem(upper + k % 2, 2) * depth + lax.rem(place_z + depth - dz, depth)

    loads = [
        pltpu.make_async_copy(src, dst, load_sem.at[n])
        for n, (src, dst) in enumerate(
            [(lat_hbm, lat_v), (wq_hbm, wq_v), (cut_hbm, cut_v), (wo_hbm, wo_v), (wqkv_hbm, wqkv_v),
             (wos_hbm, wos_v), (wup_hbm, wup_v), (wdn_hbm, wdn_v)]
        )
    ]
    brought = [
        pltpu.make_async_copy(keys_hbm, keys_v, load_sem.at[8]),
        pltpu.make_async_copy(values_hbm, values_v, load_sem.at[9]),
    ]
    for load in brought + loads[:3]:
        load.start()

    barrier = pltpu.get_barrier_semaphore()

    @pl.loop(1, chips)
    def _(k):
        pl.semaphore_signal(
            barrier, inc=1, device_id=(2 * near(k) + core, tensor), device_id_type=MESH
        )

    for d in range(1, across):
        pl.semaphore_signal(barrier, inc=1, device_id=(hist, x_peer(d)), device_id_type=MESH)
    pl.semaphore_signal(barrier, inc=1, device_id=(mate_hist, mate_tensor), device_id_type=MESH)
    pl.semaphore_signal(barrier, inc=1, device_id=(sibling, tensor), device_id_type=MESH)
    pl.semaphore_wait(barrier, chips - 1 + across - 1 + 2)

    def kv_copy(k, which, array):
        to = far(k)
        return remote(
            array.at[lax.rem(to, depth), :, column(to // depth, HD)],
            kv.at[core, which, pl.ds(pl.multiple_of(k * key_rows, key_rows), key_rows)],
            kv_ssem.at[which, k], kv_rsem.at[which, k], 2 * to + core, tensor,
        )

    def kv_own(which, array):
        return pltpu.make_async_copy(
            array.at[place_z, :, column(upper, HD)],
            kv.at[core, which, pl.ds(0, key_rows)],
            kv_rsem.at[which, 0],
        )

    for load in brought:
        load.wait()
    kv_own(0, keys_v).start()
    kv_own(1, values_v).start()

    @pl.loop(1, depth)
    def _(k):
        kv_copy(k, 0, keys_v).start()
        kv_copy(k, 1, values_v).start()

    loads[0].wait()
    loads[1].wait()
    flat = lat_v[...].reshape(rows, width)
    wide = flat.astype(F32)
    factor = lax.rsqrt(jnp.mean(wide * wide, axis=-1, keepdims=True) + EPSILON)
    query = (dot(flat, wq_v[...]) * (factor * SCALE)).astype(BF)
    qsend[...] = query.reshape(depth, lat_rows, cols)
    q_place = qbuf.at[
        pl.ds(pl.multiple_of((parity * depth + slot) * lat_rows, lat_rows), lat_rows)
    ]

    def q_copy(k):
        to = far(k)
        return remote(
            qsend.at[lax.rem(to, depth), :, column(to // depth, HD)], q_place,
            q_ssem.at[k], q_rsem.at[k], 2 * to + core, tensor,
        )

    q_own = pltpu.make_async_copy(qsend.at[place_z, :, column(upper, HD)], q_place, q_rsem.at[0])
    q_own.start()

    @pl.loop(1, chips)
    def _(k):
        q_copy(k).start()

    @pl.loop(depth, chips)
    def _(k):
        kv_copy(k, 0, keys_v).start()
        kv_copy(k, 1, values_v).start()

    for load in loads[3:]:
        load.start()

    def latent_place(row, of_half, of_core):
        return (2 * (2 * (row // lat_rows) + of_half) + of_core) * lat_rows + row % lat_rows

    loads[2].wait()
    latents = 2 * chips * lat_rows
    cut_row = cut_v[pl.ds(place_z, 1), :].astype(F32)
    for n in range(4):
        local = lax.broadcasted_iota(jnp.int32, (block_rows, 1), 0) + n % 2 * block_rows
        place = latent_place(local, n // 2, core)
        lanes = lax.broadcasted_iota(jnp.int32, (block_rows, latents), 1)
        cut_col[n * block_rows : (n + 1) * block_rows, :] = jnp.sum(
            jnp.where(lanes == place, cut_row, 0.0), axis=-1, keepdims=True
        )

    step = chips // 4
    piece = step * key_rows

    def forward(n, which):
        place = kv.at[core, which, pl.ds(n * piece, piece)]
        return remote(place, place, fw_ssem.at[which, n], fw_rsem.at[which, n], sibling, tensor)

    def take(n):
        for j in range(step):
            k = n * step + j
            if k == 0:
                kv_own(0, keys_v).wait()
                kv_own(1, values_v).wait()
            else:
                kv_copy(k, 0, keys_v).wait_recv()
                kv_copy(k, 1, values_v).wait_recv()
        forward(n, 0).start()
        forward(n, 1).start()

    def places(n, of_core):
        lane = lax.broadcasted_iota(jnp.int32, (1, piece), 1)
        base = jnp.zeros((1, piece), jnp.int32)
        for j in range(step):
            start = (2 * near(n * step + j) + of_core) * key_rows
            base = jnp.where(lane // key_rows == j, start, base)
        return (base + lane % key_rows).astype(F32)

    def cross(n, at, first, last):
        query, cut = qbuf[at, :], cut_col[at, :]
        span = slice(n * piece, (n + 1) * piece)
        scores = [
            jnp.where(
                places(n, of) < cut, dot_t(query, kv[of, 0, span, :]), MASKED
            )
            for of in range(2)
        ]
        largest = jnp.max(jnp.maximum(scores[0], scores[1]), axis=-1, keepdims=True)
        if not first:
            before = run_max[at, :]
            largest = jnp.maximum(largest, before)
        weights = [jnp.exp2(s - largest) for s in scores]
        total = jnp.sum(weights[0] + weights[1], axis=-1, keepdims=True)
        summed = dot(weights[0].astype(BF), kv[0, 1, span, :]) + dot(
            weights[1].astype(BF), kv[1, 1, span, :]
        )
        if not first:
            fade = jnp.exp2(before - largest)
            total = total + fade * run_total[at, :]
            summed = summed + fade * run_sum[at, :]
        if last:
            return (summed / total).astype(BF)
        run_max[at, :] = largest
        run_total[at, :] = total
        run_sum[at, :] = summed

    def forwarded(n):
        forward(n, 0).wait_recv()
        forward(n, 1).wait_recv()

    take(0)
    q_own.wait()

    @pl.loop(1, chips)
    def _(k):
        q_copy(k).wait_recv()

    for n in range(1, 4):
        take(n)
        forwarded(n - 1)

        @pl.loop(0, 2)
        def _(m, n=n):
            cross(n - 1, pl.ds(pl.multiple_of(m * rows, rows), rows), n == 1, False)

    lat_place = latres.at[pl.ds(pl.multiple_of(slot * lat_rows, lat_rows), lat_rows)]

    def lat_copy(k):
        to_seq = lax.rem(place_z + k, depth)
        return remote(
            lat_v.at[to_seq, :, column(tensor, cols)], lat_place,
            lat_ssem.at[k], lat_rsem.at[slot],
            2 * (holder * depth + to_seq) + core, tensor,
        )

    @pl.when(holder == upper)
    def _():
        pltpu.make_async_copy(
            lat_v.at[place_z, :, column(tensor, cols)], lat_place, lat_rsem.at[slot]
        ).start()

    @pl.when(holder != upper)
    def _():
        lat_copy(0).start()

    @pl.loop(1, depth)
    def _(k):
        lat_copy(k).start()

    def block_at(half):
        return pl.ds(half * block_rows, block_rows)

    def ctx_copy(half):
        return remote(
            ctxsend.at[block_at(half)], ctx.at[block_at(half), column(upper, HD)],
            ctx_ssem.at[half], ctx_rsem.at[half], pair, tensor,
        )

    def y_copy(phase, half, d):
        at = part_rows(half)
        return remote(
            ysend.at[phase, d, at], yrecv.at[phase, d, at],
            rsy_ssem.at[phase, half, d], rsy_rsem.at[phase, half, d], mate_hist, mate_tensor,
        )

    def x_copy(phase, half, d):
        at = part_rows(half)
        return remote(
            xsend.at[phase, d, at], xrecv.at[phase, d, at],
            rsx_ssem.at[phase, half, d], rsx_rsem.at[phase, half, d], hist, x_peer(d),
        )

    away = [2, 1, 3] if across == 4 else list(range(1, across))

    def scatter_first(phase, half, left, weight):
        at = part_rows(half)
        for d in away + [0]:
            to = (1 - lane_y) * across + lax.rem(place_x + d, across)
            ysend[phase, d, at, :] = dot(left, weight[:, column(to, cols)]).astype(BF)
            y_copy(phase, half, d).start()
        for d in away + [0]:
            partial[d, at, :] = dot(left, weight[:, column(x_peer(d), cols)])

    def scatter_second(phase, half):
        at = part_rows(half)
        for d in away:
            y_copy(phase, half, d).wait_recv()
            xsend[phase, d, at, :] = (
                partial[d, at, :] + yrecv[phase, d, at, :].astype(F32)
            ).astype(BF)
            x_copy(phase, half, d).start()

    def scatter_last(phase, half, residual):
        at = part_rows(half)
        y_copy(phase, half, 0).wait_recv()
        total = residual.astype(F32) + partial[0, at, :] + yrecv[phase, 0, at, :].astype(F32)
        for d in away:
            x_copy(phase, half, d).wait_recv()
            total = total + xrecv[phase, d, at, :].astype(F32)
        return total.astype(BF)

    def gx_copy(phase, half, d):
        at = part_rows(half)
        return remote(
            blocks.at[phase, 0, 0, at], blocks.at[phase, 0, d, at],
            agx_ssem.at[phase, half, d], agx_rsem.at[phase, half, d], hist, x_peer(d),
        )

    def gy_copy(phase, half, d):
        at = part_rows(half)
        return remote(
            blocks.at[phase, 0, d, at], blocks.at[phase, 1, d, at],
            agy_ssem.at[phase, half, d], agy_rsem.at[phase, half, d], mate_hist, mate_tensor,
        )

    def gather_start(phase, half, block):
        blocks[phase, 0, 0, part_rows(half), :] = block
        for d in away:
            gx_copy(phase, half, d).start()
        gy_copy(phase, half, 0).start()

    def gather_forward(phase, half):
        for d in away:
            gx_copy(phase, half, d).wait_recv()
            gy_copy(phase, half, d).start()

    def gather_use(phase, half, row, weights, state):
        squares, sums = state
        for d in [0] + away:
            if row:
                gy_copy(phase, half, d).wait_recv()
            source = lax.rem(lane_y + row, 2) * across + lax.rem(place_x - d + across, across)
            block = blocks[phase, row, d, part_rows(half), :]
            wide = block.astype(F32)
            squares = squares + jnp.sum(wide * wide, axis=-1, keepdims=True)
            sums = [s + dot(block, w(column(source, cols))) for s, w in zip(sums, weights)]
        return squares, sums

    def gather_norm(state):
        squares, sums = state
        factor = lax.rsqrt(squares * (1.0 / width) + EPSILON)
        return [s * factor for s in sums]

    forwarded(3)

    def last_cross(of_half, half):
        start = pl.multiple_of(of_half * rows + half * block_rows, block_rows)
        return cross(3, pl.ds(start, block_rows), False, True)

    for half in range(2):
        ctxsend[block_at(half), :] = last_cross(1 - own_half, half)
        ctx_copy(half).start()
    for half in range(2):
        ctx[block_at(half), column(upper, HD)] = last_cross(own_half, half)
    for load in loads[3:]:
        load.wait()

    def kvs_rows(p, holder_slot):
        return pl.ds((p * 4 + holder_slot) * part, part)

    def kvs_copy(which, p, source, target, device):
        return remote(
            kvs.at[which, kvs_rows(p, source)], kvs.at[which, kvs_rows(p, target)],
            kvs_ssem.at[which, p, target], kvs_rsem.at[which, p, target], device, tensor,
        )

    holders = [
        (own_half, core), (sibling_half, other_core),
        (1 - own_half, core), (1 - sibling_half, other_core),
    ]
    qkv_weights = [lambda at, n=n: wqkv_v[n, at, :] for n in range(3)]
    up_weights = [lambda at: wup_v[at, :]]
    states = {}

    def out_copy(n):
        return remote(
            enc.at[pl.ds(pl.multiple_of(n * lat_rows, lat_rows), lat_rows)],
            out_hbm.at[place_z], out_ssem.at[n], out_rsem.at[place_z],
            2 * (2 * n + own_half) + core, tensor,
        )

    def elsewhere(n):
        return 2 * n + own_half != chip

    def project_context(p):
        if p % (PARTS // 2) == 0:
            ctx_copy(p // (PARTS // 2)).wait_recv()
        scatter_first(0, p, ctx[part_rows(p), :], wo_v)

    def add_latents(p):
        for k in range(p * depth // PARTS, (p + 1) * depth // PARTS):
            lat_slot = latres.at[pl.ds(k * lat_rows, lat_rows)]
            pltpu.make_async_copy(lat_slot, lat_slot, lat_rsem.at[k]).wait()
        gather_start(0, p, scatter_last(0, p, latres[part_rows(p), :]))

    def gather_near(phase, p, weights):
        gather_forward(phase, p)
        states[phase, p] = gather_use(phase, p, 0, weights, (0.0, [0.0 for _ in weights]))

    def project_self(p):
        self_q, self_k, self_v = gather_norm(gather_use(0, p, 1, qkv_weights, states[0, p]))
        kvs[0, kvs_rows(p, 0), :] = self_k.astype(BF)
        kvs[1, kvs_rows(p, 0), :] = self_v.astype(BF)
        for which in range(2):
            kvs_copy(which, p, 0, 2, pair).start()
        for which in range(2):
            kvs_copy(which, p, 0, 1, sibling).start()
        qself[part_rows(p), :] = (self_q * SCALE).astype(BF)

    def share(p):
        for which in range(2):
            kvs_copy(which, p, 0, 2, pair).wait_recv()
            kvs_copy(which, p, 2, 3, sibling).start()

    def attend_self(p):
        for which in range(2):
            kvs_copy(which, p, 0, 1, sibling).wait_recv()
            kvs_copy(which, p, 2, 3, sibling).wait_recv()
        own_place = latent_place(
            lax.broadcasted_iota(jnp.int32, (part, 1), 0) + p * part, own_half, core
        )
        seen = (p + 1) * 4 * part
        lane = lax.broadcasted_iota(jnp.int32, (1, seen), 1)
        by = lane // part % 4
        row = lane // (4 * part) * part + lane % part
        place = latent_place(row, *holders[0])
        for n in range(1, 4):
            place = jnp.where(by == n, latent_place(row, *holders[n]), place)
        visible = place <= own_place
        for h in range(cols // HD):
            at = slice(h * HD, (h + 1) * HD)
            mixed[part_rows(p), at] = attend(
                qself[part_rows(p), at], [(kvs[0, :seen, at], kvs[1, :seen, at], visible)]
            )
        scatter_first(1, p, mixed[part_rows(p), :], wos_v)

    def add_first(p):
        gather_start(1, p, scatter_last(1, p, blocks[0, 0, 0, part_rows(p), :]))

    def mlp(p):
        (raised,) = gather_norm(gather_use(1, p, 1, up_weights, states[1, p]))
        scatter_first(2, p, jax.nn.gelu(raised).astype(BF), wdn_v)

    def send_back(p):
        enc[part_rows(p), :] = scatter_last(2, p, blocks[1, 0, 0, part_rows(p), :])

        @pl.loop(p * depth // PARTS, (p + 1) * depth // PARTS)
        def _(n):
            @pl.when(elsewhere(n))
            def _():
                out_copy(n).start()

    steps = [
        project_context,
        lambda p: scatter_second(0, p),
        add_latents,
        lambda p: gather_near(0, p, qkv_weights),
        project_self,
        share,
        attend_self,
        lambda p: scatter_second(1, p),
        add_first,
        lambda p: gather_near(1, p, up_weights),
        mlp,
        lambda p: scatter_second(2, p),
        send_back,
    ]
    for _, p, n in sorted((n + LAG * p, p, n) for n in range(len(steps)) for p in range(PARTS)):
        steps[n](p)

    @pl.when(parity == own_half)
    def _():
        pltpu.make_async_copy(
            enc.at[pl.ds(pl.multiple_of(slot * lat_rows, lat_rows), lat_rows)],
            out_hbm.at[place_z], out_rsem.at[place_z],
        ).start()

    @pl.loop(1, chips)
    def _(k):
        kv_copy(k, 0, keys_v).wait_send()
        kv_copy(k, 1, values_v).wait_send()
        q_copy(k).wait_send()

    @pl.when(holder != upper)
    def _():
        lat_copy(0).wait_send()

    @pl.loop(1, depth)
    def _(k):
        lat_copy(k).wait_send()

    for n in range(4):
        forward(n, 0).wait_send()
        forward(n, 1).wait_send()
    for half in range(2):
        ctx_copy(half).wait_send()
    for half in range(PARTS):
        for phase in range(3):
            for d in range(across):
                y_copy(phase, half, d).wait_send()
            for d in away:
                x_copy(phase, half, d).wait_send()
        for phase in range(2):
            for d in range(across):
                gy_copy(phase, half, d).wait_send()
            for d in away:
                gx_copy(phase, half, d).wait_send()
        for which in range(2):
            kvs_copy(which, half, 0, 2, pair).wait_send()
            kvs_copy(which, half, 0, 1, sibling).wait_send()
            kvs_copy(which, half, 2, 3, sibling).wait_send()

    for n in range(depth):
        pltpu.make_async_copy(out_hbm.at[n], out_hbm.at[n], out_rsem.at[n]).wait()

    @pl.loop(0, depth)
    def _(n):
        @pl.when(elsewhere(n))
        def _():
            out_copy(n).wait_send()


def body(latents, keys, values, cutoff, w_q, w_o, w_qkv, w_os, w_up, w_down):
    seqs, lat_rows, width = latents.shape
    key_rows, cols = keys.shape[1:]
    chips = lax.axis_size("hist") // 2
    tensors = lax.axis_size("tensor")
    across = tensors // 2
    depth = chips // 2
    rows = seqs * lat_rows

    def vmem(*shape):
        return pltpu.VMEM(shape, BF)

    def wide(*shape):
        return pltpu.VMEM(shape, F32)

    dma = pltpu.SemaphoreType.DMA
    hbm = pl.BlockSpec(memory_space=pltpu.HBM)
    return pl.pallas_call(
        functools.partial(step_kernel, (chips, tensors, lat_rows, key_rows, width)),
        out_shape=jax.ShapeDtypeStruct((seqs, lat_rows, cols), BF),
        in_specs=[hbm] * 10,
        out_specs=hbm,
        scratch_shapes=[
            vmem(*keys.shape), vmem(*values.shape),
            vmem(*latents.shape), pltpu.VMEM(cutoff.shape, jnp.int32),
            vmem(*w_q.shape), vmem(*w_o.shape), vmem(*w_qkv.shape),
            vmem(*w_os.shape), vmem(*w_up.shape), vmem(*w_down.shape),
            vmem(2, 2, chips * key_rows, HD),
            vmem(seqs, lat_rows, cols),
            vmem(chips * lat_rows, HD),
            wide(chips * lat_rows, 1), wide(chips * lat_rows, 1), wide(chips * lat_rows, 1),
            wide(chips * lat_rows, HD),
            vmem(rows, cols),
            vmem(rows, HD),
            vmem(rows, cols),
            wide(across, rows, cols),
            vmem(3, across, rows, cols), vmem(3, across, rows, cols),
            vmem(3, across, rows, cols), vmem(3, across, rows, cols),
            vmem(2, 2, across, rows, cols),
            vmem(rows, cols),
            vmem(2, 4 * rows, cols),
            vmem(rows, cols),
            vmem(rows, cols),
            dma((10,)),
            dma((2, chips)), dma((2, chips)),
            dma((2, 4)), dma((2, 4)),
            dma((chips,)), dma((chips,)),
            dma((depth,)), dma((depth,)),
            dma((2,)), dma((2,)),
            *[dma((3, PARTS, across))] * 4,
            *[dma((2, PARTS, across))] * 4,
            *[dma((2, PARTS, 4))] * 2,
            dma((depth,)), dma((depth,)),
        ],
        compiler_params=pltpu.CompilerParams(
            collective_id=0, has_side_effects=True, vmem_limit_bytes=60 * 1024 * 1024
        ),
        cost_estimate=pl.CostEstimate(
            flops=8 * rows * width * cols * 5, bytes_accessed=12 * 1024 * 1024, transcendentals=0
        ),
    )(latents, keys, values, cutoff, w_q, w_o, w_qkv, w_os, w_up, w_down)


def solution(mesh):
    placed = (
        P(None, "hist", None),
        P(None, "hist", "tensor"),
        P(None, "hist", "tensor"),
        P(),
        P(None, "tensor"),
        P("tensor", None),
        P(None, None, "tensor"),
        P("tensor", None),
        P(None, "tensor"),
        P("tensor", None),
    )
    return jax.shard_map(
        body, mesh=mesh, in_specs=placed, out_specs=P(None, "hist", "tensor"), check_vma=False
    )
```

```python
import functools
import math

import jax
import jax.numpy as jnp
from jax import lax
from jax.experimental import pallas as pl
from jax.experimental.pallas import tpu as pltpu
from jax.sharding import PartitionSpec as P

HD = 128
EPSILON = 1e-06
MASKED = -1e30
MESH = pl.DeviceIdType.MESH
BF = jnp.bfloat16
F32 = jnp.float32
PARTS = 4
LAG = 0.67
SCALE = math.log2(math.e) / math.sqrt(HD)


def dot(left, right):
    return jnp.dot(left, right, preferred_element_type=F32)


def dot_t(left, right):
    return lax.dot_general(left, right, (((1,), (1,)), ((), ())), preferred_element_type=F32)


def remote(src, dst, send_sem, recv_sem, hist, tensor):
    return pltpu.make_async_remote_copy(
        src_ref=src,
        dst_ref=dst,
        send_sem=send_sem,
        recv_sem=recv_sem,
        device_id=(hist, tensor),
        device_id_type=MESH,
    )


def attend(query, pieces):
    scores = [jnp.where(seen, dot_t(query, keys), MASKED) for keys, _, seen in pieces]
    largest = functools.reduce(jnp.maximum, [jnp.max(s, axis=-1, keepdims=True) for s in scores])
    total = jnp.zeros_like(largest)
    summed = jnp.zeros((query.shape[0], HD), F32)
    for score, (_, values, _) in zip(scores, pieces):
        weights = jnp.exp2(score - largest)
        total = total + jnp.sum(weights, axis=-1, keepdims=True)
        summed = summed + dot(weights.astype(BF), values)
    return (summed / total).astype(BF)


def step_kernel(
    sizes,
    lat_hbm, keys_hbm, values_hbm, cut_hbm, wq_hbm, wo_hbm, wqkv_hbm, wos_hbm, wup_hbm, wdn_hbm,
    out_hbm,
    keys_v, values_v, lat_v, cut_v, wq_v, wo_v, wqkv_v, wos_v, wup_v, wdn_v,
    kv, qsend, qbuf, cut_col, run_max, run_total, run_sum, latres, ctxsend, ctx,
    partial, ysend, yrecv, xsend, xrecv, blocks, qself, kvs, mixed, enc,
    load_sem, kv_ssem, kv_rsem, fw_ssem, fw_rsem, q_ssem, q_rsem, lat_ssem, lat_rsem,
    ctx_ssem, ctx_rsem, rsy_ssem, rsy_rsem, rsx_ssem, rsx_rsem, agy_ssem, agy_rsem, agx_ssem, agx_rsem,
    kvs_ssem, kvs_rsem, out_ssem, out_rsem,
):
    chips, tensors, lat_rows, key_rows, width = sizes
    depth = chips // 2
    rows = depth * lat_rows
    part = rows // PARTS
    block_rows = rows // 2
    cols = width // tensors
    across = tensors // 2
    hist = lax.axis_index("hist")
    tensor = lax.axis_index("tensor")
    core = lax.rem(hist, 2)
    chip = hist // 2
    upper = chip // depth
    place_z = lax.rem(chip, depth)
    lane_y = tensor // across
    place_x = lax.rem(tensor, across)
    other_core = 1 - core
    sibling = 2 * chip + other_core
    pair = 2 * ((1 - upper) * depth + place_z) + core
    pair_other = 2 * ((1 - upper) * depth + place_z) + other_core
    twist = core * lane_y
    own_half = lax.rem(upper + twist, 2)
    sibling_half = lax.rem(upper + other_core * lane_y, 2)
    parity = lax.rem(chip, 2)
    holder = lax.rem(parity + twist, 2)
    slot = chip // 2
    mate_hist = 2 * (lax.rem(upper + core, 2) * depth + place_z) + core
    mate_tensor = (1 - lane_y) * across + place_x

    def column(index, size):
        return pl.ds(pl.multiple_of(index * size, size), size)

    def part_rows(half):
        return pl.ds(half * part, part)

    def x_peer(d):
        return lane_y * across + lax.rem(place_x + d, across)

    def far(k):
        j = k // 2
        dz = ((j + 1) // 2) * (2 * (j % 2) - 1)
        return lax.rem(upper + k % 2, 2) * depth + lax.rem(place_z + depth + dz, depth)

    def near(k):
        j = k // 2
        dz = ((j + 1) // 2) * (2 * (j % 2) - 1)
        return lax.rem(upper + k % 2, 2) * depth + lax.rem(place_z + depth - dz, depth)

    loads = [
        pltpu.make_async_copy(src, dst, load_sem.at[n])
        for n, (src, dst) in enumerate(
            [(lat_hbm, lat_v), (wq_hbm, wq_v), (cut_hbm, cut_v), (wo_hbm, wo_v), (wqkv_hbm, wqkv_v),
             (wos_hbm, wos_v), (wup_hbm, wup_v), (wdn_hbm, wdn_v)]
        )
    ]
    brought = [
        pltpu.make_async_copy(keys_hbm, keys_v, load_sem.at[8]),
        pltpu.make_async_copy(values_hbm, values_v, load_sem.at[9]),
    ]
    for load in brought + loads[:3]:
        load.start()

    barrier = pltpu.get_barrier_semaphore()

    @pl.loop(1, chips)
    def _(k):
        pl.semaphore_signal(
            barrier, inc=1, device_id=(2 * near(k) + core, tensor), device_id_type=MESH
        )

    for d in range(1, across):
        pl.semaphore_signal(barrier, inc=1, device_id=(hist, x_peer(d)), device_id_type=MESH)
    pl.semaphore_signal(barrier, inc=1, device_id=(mate_hist, mate_tensor), device_id_type=MESH)
    pl.semaphore_signal(barrier, inc=1, device_id=(sibling, tensor), device_id_type=MESH)
    pl.semaphore_signal(barrier, inc=1, device_id=(pair_other, tensor), device_id_type=MESH)
    pl.semaphore_wait(barrier, chips - 1 + across - 1 + 3)

    def kv_copy(k, which, array):
        to = far(k)
        return remote(
            array.at[lax.rem(to, depth), :, column(to // depth, HD)],
            kv.at[core, which, pl.ds(pl.multiple_of(k * key_rows, key_rows), key_rows)],
            kv_ssem.at[which, k], kv_rsem.at[which, k], 2 * to + core, tensor,
        )

    def kv_own(which, array):
        return pltpu.make_async_copy(
            array.at[place_z, :, column(upper, HD)],
            kv.at[core, which, pl.ds(0, key_rows)],
            kv_rsem.at[which, 0],
        )

    for load in brought:
        load.wait()
    kv_own(0, keys_v).start()
    kv_own(1, values_v).start()

    @pl.loop(1, depth)
    def _(k):
        kv_copy(k, 0, keys_v).start()
        kv_copy(k, 1, values_v).start()

    loads[0].wait()
    loads[1].wait()
    flat = lat_v[...].reshape(rows, width)
    wide = flat.astype(F32)
    factor = lax.rsqrt(jnp.mean(wide * wide, axis=-1, keepdims=True) + EPSILON)
    query = (dot(flat, wq_v[...]) * (factor * SCALE)).astype(BF)
    qsend[...] = query.reshape(depth, lat_rows, cols)
    q_place = qbuf.at[
        pl.ds(pl.multiple_of((parity * depth + slot) * lat_rows, lat_rows), lat_rows)
    ]

    def q_copy(k):
        to = far(k)
        return remote(
            qsend.at[lax.rem(to, depth), :, column(to // depth, HD)], q_place,
            q_ssem.at[k], q_rsem.at[k], 2 * to + core, tensor,
        )

    q_own = pltpu.make_async_copy(qsend.at[place_z, :, column(upper, HD)], q_place, q_rsem.at[0])
    q_own.start()

    @pl.loop(1, chips)
    def _(k):
        q_copy(k).start()

    @pl.loop(depth, chips)
    def _(k):
        kv_copy(k, 0, keys_v).start()
        kv_copy(k, 1, values_v).start()

    for load in loads[3:]:
        load.start()

    def latent_place(row, of_half, of_core):
        return (2 * (2 * (row // lat_rows) + of_half) + of_core) * lat_rows + row % lat_rows

    loads[2].wait()
    latents = 2 * chips * lat_rows
    cut_row = cut_v[pl.ds(place_z, 1), :].astype(F32)
    for n in range(4):
        local = lax.broadcasted_iota(jnp.int32, (block_rows, 1), 0) + n % 2 * block_rows
        place = latent_place(local, n // 2, core)
        lanes = lax.broadcasted_iota(jnp.int32, (block_rows, latents), 1)
        cut_col[n * block_rows : (n + 1) * block_rows, :] = jnp.sum(
            jnp.where(lanes == place, cut_row, 0.0), axis=-1, keepdims=True
        )

    step = chips // 4
    piece = step * key_rows

    def forward(n, which):
        place = kv.at[core, which, pl.ds(n * piece, piece)]
        return remote(place, place, fw_ssem.at[which, n], fw_rsem.at[which, n], sibling, tensor)

    def take(n):
        for j in range(step):
            k = n * step + j
            if k == 0:
                kv_own(0, keys_v).wait()
                kv_own(1, values_v).wait()
            else:
                kv_copy(k, 0, keys_v).wait_recv()
                kv_copy(k, 1, values_v).wait_recv()
        forward(n, 0).start()
        forward(n, 1).start()

    def places(n, of_core):
        lane = lax.broadcasted_iota(jnp.int32, (1, piece), 1)
        base = jnp.zeros((1, piece), jnp.int32)
        for j in range(step):
            start = (2 * near(n * step + j) + of_core) * key_rows
            base = jnp.where(lane // key_rows == j, start, base)
        return (base + lane % key_rows).astype(F32)

    def cross(n, at, first, last):
        query, cut = qbuf[at, :], cut_col[at, :]
        span = slice(n * piece, (n + 1) * piece)
        scores = [
            jnp.where(
                places(n, of) < cut, dot_t(query, kv[of, 0, span, :]), MASKED
            )
            for of in range(2)
        ]
        largest = jnp.max(jnp.maximum(scores[0], scores[1]), axis=-1, keepdims=True)
        if not first:
            before = run_max[at, :]
            largest = jnp.maximum(largest, before)
        weights = [jnp.exp2(s - largest) for s in scores]
        total = jnp.sum(weights[0] + weights[1], axis=-1, keepdims=True)
        summed = dot(weights[0].astype(BF), kv[0, 1, span, :]) + dot(
            weights[1].astype(BF), kv[1, 1, span, :]
        )
        if not first:
            fade = jnp.exp2(before - largest)
            total = total + fade * run_total[at, :]
            summed = summed + fade * run_sum[at, :]
        if last:
            return (summed / total).astype(BF)
        run_max[at, :] = largest
        run_total[at, :] = total
        run_sum[at, :] = summed

    def forwarded(n):
        forward(n, 0).wait_recv()
        forward(n, 1).wait_recv()

    take(0)
    q_own.wait()

    @pl.loop(1, chips)
    def _(k):
        q_copy(k).wait_recv()

    for n in range(1, 4):
        take(n)
        forwarded(n - 1)

        @pl.loop(0, 2)
        def _(m, n=n):
            cross(n - 1, pl.ds(pl.multiple_of(m * rows, rows), rows), n == 1, False)

    lat_place = latres.at[pl.ds(pl.multiple_of(slot * lat_rows, lat_rows), lat_rows)]

    def lat_copy(k):
        to_seq = lax.rem(place_z + k, depth)
        return remote(
            lat_v.at[to_seq, :, column(tensor, cols)], lat_place,
            lat_ssem.at[k], lat_rsem.at[slot],
            2 * (holder * depth + to_seq) + core, tensor,
        )

    @pl.when(holder == upper)
    def _():
        pltpu.make_async_copy(
            lat_v.at[place_z, :, column(tensor, cols)], lat_place, lat_rsem.at[slot]
        ).start()

    @pl.when(holder != upper)
    def _():
        lat_copy(0).start()

    @pl.loop(1, depth)
    def _(k):
        lat_copy(k).start()

    def block_at(half):
        return pl.ds(half * block_rows, block_rows)

    def ctx_copy(half):
        return remote(
            ctxsend.at[block_at(half)], ctx.at[block_at(half), column(upper, HD)],
            ctx_ssem.at[half], ctx_rsem.at[half], pair, tensor,
        )

    def y_copy(phase, half, d):
        at = part_rows(half)
        return remote(
            ysend.at[phase, d, at], yrecv.at[phase, d, at],
            rsy_ssem.at[phase, half, d], rsy_rsem.at[phase, half, d], mate_hist, mate_tensor,
        )

    def x_copy(phase, half, d):
        at = part_rows(half)
        return remote(
            xsend.at[phase, d, at], xrecv.at[phase, d, at],
            rsx_ssem.at[phase, half, d], rsx_rsem.at[phase, half, d], hist, x_peer(d),
        )

    away = [2, 1, 3] if across == 4 else list(range(1, across))

    def scatter_first(phase, half, left, weight):
        at = part_rows(half)
        for d in away + [0]:
            to = (1 - lane_y) * across + lax.rem(place_x + d, across)
            ysend[phase, d, at, :] = dot(left, weight[:, column(to, cols)]).astype(BF)
            y_copy(phase, half, d).start()
        for d in away + [0]:
            partial[d, at, :] = dot(left, weight[:, column(x_peer(d), cols)])

    def scatter_second(phase, half):
        at = part_rows(half)
        for d in away:
            y_copy(phase, half, d).wait_recv()
            xsend[phase, d, at, :] = (
                partial[d, at, :] + yrecv[phase, d, at, :].astype(F32)
            ).astype(BF)
            x_copy(phase, half, d).start()

    def scatter_last(phase, half, residual):
        at = part_rows(half)
        y_copy(phase, half, 0).wait_recv()
        total = residual.astype(F32) + partial[0, at, :] + yrecv[phase, 0, at, :].astype(F32)
        for d in away:
            x_copy(phase, half, d).wait_recv()
            total = total + xrecv[phase, d, at, :].astype(F32)
        return total.astype(BF)

    def gx_copy(phase, half, d):
        at = part_rows(half)
        return remote(
            blocks.at[phase, 0, 0, at], blocks.at[phase, 0, d, at],
            agx_ssem.at[phase, half, d], agx_rsem.at[phase, half, d], hist, x_peer(d),
        )

    def gy_copy(phase, half, d):
        at = part_rows(half)
        return remote(
            blocks.at[phase, 0, d, at], blocks.at[phase, 1, d, at],
            agy_ssem.at[phase, half, d], agy_rsem.at[phase, half, d], mate_hist, mate_tensor,
        )

    def gather_start(phase, half, block):
        blocks[phase, 0, 0, part_rows(half), :] = block
        for d in away:
            gx_copy(phase, half, d).start()
        gy_copy(phase, half, 0).start()

    def gather_forward(phase, half):
        for d in away:
            gx_copy(phase, half, d).wait_recv()
            gy_copy(phase, half, d).start()

    def gather_use(phase, half, row, weights, state):
        squares, sums = state
        for d in [0] + away:
            if row:
                gy_copy(phase, half, d).wait_recv()
            source = lax.rem(lane_y + row, 2) * across + lax.rem(place_x - d + across, across)
            block = blocks[phase, row, d, part_rows(half), :]
            wide = block.astype(F32)
            squares = squares + jnp.sum(wide * wide, axis=-1, keepdims=True)
            sums = [s + dot(block, w(column(source, cols))) for s, w in zip(sums, weights)]
        return squares, sums

    def gather_norm(state):
        squares, sums = state
        factor = lax.rsqrt(squares * (1.0 / width) + EPSILON)
        return [s * factor for s in sums]

    forwarded(3)

    def last_cross(of_half, half):
        start = pl.multiple_of(of_half * rows + half * block_rows, block_rows)
        return cross(3, pl.ds(start, block_rows), False, True)

    for half in range(2):
        ctxsend[block_at(half), :] = last_cross(1 - own_half, half)
        ctx_copy(half).start()
    for half in range(2):
        ctx[block_at(half), column(upper, HD)] = last_cross(own_half, half)
    for load in loads[3:]:
        load.wait()

    def kvs_rows(p, holder_slot):
        return pl.ds((p * 4 + holder_slot) * part, part)

    def kvs_copy(which, p, source, target, device):
        return remote(
            kvs.at[which, kvs_rows(p, source)], kvs.at[which, kvs_rows(p, target)],
            kvs_ssem.at[which, p, target], kvs_rsem.at[which, p, target], device, tensor,
        )

    holders = [
        (own_half, core), (sibling_half, other_core),
        (1 - own_half, core), (1 - sibling_half, other_core),
    ]
    qkv_weights = [lambda at, n=n: wqkv_v[n, at, :] for n in range(3)]
    up_weights = [lambda at: wup_v[at, :]]
    states = {}

    def out_copy(n):
        return remote(
            enc.at[pl.ds(pl.multiple_of(n * lat_rows, lat_rows), lat_rows)],
            out_hbm.at[place_z], out_ssem.at[n], out_rsem.at[place_z],
            2 * (2 * n + own_half) + core, tensor,
        )

    def elsewhere(n):
        return 2 * n + own_half != chip

    def project_context(p):
        if p % (PARTS // 2) == 0:
            ctx_copy(p // (PARTS // 2)).wait_recv()
        scatter_first(0, p, ctx[part_rows(p), :], wo_v)

    def add_latents(p):
        for k in range(p * depth // PARTS, (p + 1) * depth // PARTS):
            lat_slot = latres.at[pl.ds(k * lat_rows, lat_rows)]
            pltpu.make_async_copy(lat_slot, lat_slot, lat_rsem.at[k]).wait()
        gather_start(0, p, scatter_last(0, p, latres[part_rows(p), :]))

    def gather_near(phase, p, weights):
        gather_forward(phase, p)
        states[phase, p] = gather_use(phase, p, 0, weights, (0.0, [0.0 for _ in weights]))

    def project_self(p):
        self_q, self_k, self_v = gather_norm(gather_use(0, p, 1, qkv_weights, states[0, p]))
        kvs[0, kvs_rows(p, 0), :] = self_k.astype(BF)
        kvs[1, kvs_rows(p, 0), :] = self_v.astype(BF)
        for which in range(2):
            kvs_copy(which, p, 0, 2, pair).start()
            kvs_copy(which, p, 0, 3, pair_other).start()
        for which in range(2):
            kvs_copy(which, p, 0, 1, sibling).start()
        qself[part_rows(p), :] = (self_q * SCALE).astype(BF)

    def attend_self(p):
        for which in range(2):
            kvs_copy(which, p, 0, 1, sibling).wait_recv()
            kvs_copy(which, p, 0, 2, pair).wait_recv()
            kvs_copy(which, p, 0, 3, pair_other).wait_recv()
        own_place = latent_place(
            lax.broadcasted_iota(jnp.int32, (part, 1), 0) + p * part, own_half, core
        )
        seen = (p + 1) * 4 * part
        lane = lax.broadcasted_iota(jnp.int32, (1, seen), 1)
        by = lane // part % 4
        row = lane // (4 * part) * part + lane % part
        place = latent_place(row, *holders[0])
        for n in range(1, 4):
            place = jnp.where(by == n, latent_place(row, *holders[n]), place)
        visible = place <= own_place
        for h in range(cols // HD):
            at = slice(h * HD, (h + 1) * HD)
            mixed[part_rows(p), at] = attend(
                qself[part_rows(p), at], [(kvs[0, :seen, at], kvs[1, :seen, at], visible)]
            )
        scatter_first(1, p, mixed[part_rows(p), :], wos_v)

    def add_first(p):
        gather_start(1, p, scatter_last(1, p, blocks[0, 0, 0, part_rows(p), :]))

    def mlp(p):
        (raised,) = gather_norm(gather_use(1, p, 1, up_weights, states[1, p]))
        scatter_first(2, p, jax.nn.gelu(raised).astype(BF), wdn_v)

    def send_back(p):
        enc[part_rows(p), :] = scatter_last(2, p, blocks[1, 0, 0, part_rows(p), :])

        @pl.loop(p * depth // PARTS, (p + 1) * depth // PARTS)
        def _(n):
            @pl.when(elsewhere(n))
            def _():
                out_copy(n).start()

    steps = [
        project_context,
        lambda p: scatter_second(0, p),
        add_latents,
        lambda p: gather_near(0, p, qkv_weights),
        project_self,
        attend_self,
        lambda p: scatter_second(1, p),
        add_first,
        lambda p: gather_near(1, p, up_weights),
        mlp,
        lambda p: scatter_second(2, p),
        send_back,
    ]
    for _, p, n in sorted((n + LAG * p, p, n) for n in range(len(steps)) for p in range(PARTS)):
        steps[n](p)

    @pl.when(parity == own_half)
    def _():
        pltpu.make_async_copy(
            enc.at[pl.ds(pl.multiple_of(slot * lat_rows, lat_rows), lat_rows)],
            out_hbm.at[place_z], out_rsem.at[place_z],
        ).start()

    @pl.loop(1, chips)
    def _(k):
        kv_copy(k, 0, keys_v).wait_send()
        kv_copy(k, 1, values_v).wait_send()
        q_copy(k).wait_send()

    @pl.when(holder != upper)
    def _():
        lat_copy(0).wait_send()

    @pl.loop(1, depth)
    def _(k):
        lat_copy(k).wait_send()

    for n in range(4):
        forward(n, 0).wait_send()
        forward(n, 1).wait_send()
    for half in range(2):
        ctx_copy(half).wait_send()
    for half in range(PARTS):
        for phase in range(3):
            for d in range(across):
                y_copy(phase, half, d).wait_send()
            for d in away:
                x_copy(phase, half, d).wait_send()
        for phase in range(2):
            for d in range(across):
                gy_copy(phase, half, d).wait_send()
            for d in away:
                gx_copy(phase, half, d).wait_send()
        for which in range(2):
            kvs_copy(which, half, 0, 2, pair).wait_send()
            kvs_copy(which, half, 0, 1, sibling).wait_send()
            kvs_copy(which, half, 0, 3, pair_other).wait_send()

    for n in range(depth):
        pltpu.make_async_copy(out_hbm.at[n], out_hbm.at[n], out_rsem.at[n]).wait()

    @pl.loop(0, depth)
    def _(n):
        @pl.when(elsewhere(n))
        def _():
            out_copy(n).wait_send()


def body(latents, keys, values, cutoff, w_q, w_o, w_qkv, w_os, w_up, w_down):
    seqs, lat_rows, width = latents.shape
    key_rows, cols = keys.shape[1:]
    chips = lax.axis_size("hist") // 2
    tensors = lax.axis_size("tensor")
    across = tensors // 2
    depth = chips // 2
    rows = seqs * lat_rows

    def vmem(*shape):
        return pltpu.VMEM(shape, BF)

    def wide(*shape):
        return pltpu.VMEM(shape, F32)

    dma = pltpu.SemaphoreType.DMA
    hbm = pl.BlockSpec(memory_space=pltpu.HBM)
    return pl.pallas_call(
        functools.partial(step_kernel, (chips, tensors, lat_rows, key_rows, width)),
        out_shape=jax.ShapeDtypeStruct((seqs, lat_rows, cols), BF),
        in_specs=[hbm] * 10,
        out_specs=hbm,
        scratch_shapes=[
            vmem(*keys.shape), vmem(*values.shape),
            vmem(*latents.shape), pltpu.VMEM(cutoff.shape, jnp.int32),
            vmem(*w_q.shape), vmem(*w_o.shape), vmem(*w_qkv.shape),
            vmem(*w_os.shape), vmem(*w_up.shape), vmem(*w_down.shape),
            vmem(2, 2, chips * key_rows, HD),
            vmem(seqs, lat_rows, cols),
            vmem(chips * lat_rows, HD),
            wide(chips * lat_rows, 1), wide(chips * lat_rows, 1), wide(chips * lat_rows, 1),
            wide(chips * lat_rows, HD),
            vmem(rows, cols),
            vmem(rows, HD),
            vmem(rows, cols),
            wide(across, rows, cols),
            vmem(3, across, rows, cols), vmem(3, across, rows, cols),
            vmem(3, across, rows, cols), vmem(3, across, rows, cols),
            vmem(2, 2, across, rows, cols),
            vmem(rows, cols),
            vmem(2, 4 * rows, cols),
            vmem(rows, cols),
            vmem(rows, cols),
            dma((10,)),
            dma((2, chips)), dma((2, chips)),
            dma((2, 4)), dma((2, 4)),
            dma((chips,)), dma((chips,)),
            dma((depth,)), dma((depth,)),
            dma((2,)), dma((2,)),
            *[dma((3, PARTS, across))] * 4,
            *[dma((2, PARTS, across))] * 4,
            *[dma((2, PARTS, 4))] * 2,
            dma((depth,)), dma((depth,)),
        ],
        compiler_params=pltpu.CompilerParams(
            collective_id=0, has_side_effects=True, vmem_limit_bytes=60 * 1024 * 1024
        ),
        cost_estimate=pl.CostEstimate(
            flops=8 * rows * width * cols * 5, bytes_accessed=12 * 1024 * 1024, transcendentals=0
        ),
    )(latents, keys, values, cutoff, w_q, w_o, w_qkv, w_os, w_up, w_down)


def solution(mesh):
    placed = (
        P(None, "hist", None),
        P(None, "hist", "tensor"),
        P(None, "hist", "tensor"),
        P(),
        P(None, "tensor"),
        P("tensor", None),
        P(None, None, "tensor"),
        P("tensor", None),
        P(None, "tensor"),
        P("tensor", None),
    )
    return jax.shard_map(
        body, mesh=mesh, in_specs=placed, out_specs=P(None, "hist", "tensor"), check_vma=False
    )
```
